512 devices in a mesh: src: 32 (over y, z_hi), rcv: 16 (over z_lo, x, core).
Axes of the slice: x: 4, y: 8, z: 8 (z_hi: 4, z_lo: 2; z = z_hi * 2 + z_lo), core: 2. Of those that a mesh axis runs over, the one named last changes fastest.
Arguments:
- traces: bfloat16 [32, 16, 256, 2048], P('src', 'rcv'), may hold values from -6 to 6
- source_ids: int32 [32, 16, 256], P('src', 'rcv'), may hold values from 0 to 31
- receiver_ids: int32 [32, 16, 256], P('src', 'rcv'), may hold values from 0 to 31
- offset_ids: int32 [32, 16, 256], P('src', 'rcv'), may hold values from 0 to 63
- receiver_init: float32 [512, 1024], P('rcv'), may hold values from -6 to 6
- offset_init: float32 [64, 1024], replicated, may hold values from -6 to 6
Outputs:
- source_terms: float32 [1024, 1024], P('src')
- receiver_terms: float32 [512, 1024], P('rcv')
- offset_terms: float32 [64, 1024], replicated
- residual: float32 [32, 16, 256, 1024], P('src', 'rcv')
The draws below stay inside these ranges and needn't reach their ends.
All inputs are finite; a program needn't handle non-finite values.
Results may differ from the reference program's by a relative error of at most 0.0034.
Values sent between devices are 32-bit elements; how exact they have to be, the bound alone decides.
A program may use at most 64 MiB of HBM per device.

```python
import jax
import jax.numpy as jnp
from jax import lax

NS = 2048
NF = 1024
TR_DEV = 256
NSRC_DEV = 32
NRCV_DEV = 32
NOFF = 64
SRC_BLOCKS = 32
RCV_BLOCKS = 16
RECEIVERS = 512


def place_ends(result, stream_key, smallest, top_value):
    spot = [jax.random.randint(jax.random.fold_in(stream_key, axis), (), 0, length) for axis, length in enumerate(result.shape)]
    main_axis = result.shape.index(max(result.shape))
    next_to = spot[:main_axis] + [(spot[main_axis] + 1) % result.shape[main_axis]] + spot[main_axis + 1:]
    return result.at[tuple(spot)].set(smallest).at[tuple(next_to)].set(top_value)


def steps_of(rng, shape, shards, smallest, top_value):
    level, own = 1.0, jax.random.fold_in(rng, 6)
    for dim, parts in shards:
        draws = jnp.exp(jax.random.uniform(jax.random.fold_in(own, dim), (parts,), jnp.float32, smallest / len(shards), top_value / len(shards)))
        level = level * jnp.repeat(draws, shape[dim] // parts).reshape([-1 if axis == dim else 1 for axis in range(len(shape))])
    return level


def centred(key, extent, scale, most, split=(), kind=jnp.bfloat16):
    array = jax.random.normal(key, extent, jnp.float32) * scale
    if len(split) > 0:
        array = steps_of(key, extent, split, -0.22, 0.18) * array
    return jnp.clip(array, min=-most, max=most).astype(kind)


def setup_inputs(seed: int = 0) -> dict:
    key_list = jax.random.split(jax.random.key(seed), 7)
    traces = centred(key_list[0], (SRC_BLOCKS, RCV_BLOCKS, TR_DEV, NS), 1.0, 6.0, ((0, 32), (1, 16)))
    source_ids = place_ends(jax.random.randint(key_list[1], (SRC_BLOCKS, RCV_BLOCKS, TR_DEV), 0, NSRC_DEV), jax.random.fold_in(key_list[1], 1), 0, NSRC_DEV - 1).astype(jnp.int32)
    receiver_ids = place_ends(jax.random.randint(key_list[2], (SRC_BLOCKS, RCV_BLOCKS, TR_DEV), 0, NRCV_DEV), jax.random.fold_in(key_list[2], 1), 0, NRCV_DEV - 1).astype(jnp.int32)
    offset_ids = place_ends(jax.random.randint(key_list[3], (SRC_BLOCKS, RCV_BLOCKS, TR_DEV), 0, NOFF), jax.random.fold_in(key_list[3], 1), 0, NOFF - 1).astype(jnp.int32)
    receiver_init = centred(key_list[4], (RECEIVERS, NF), 1.0, 6.0, ((0, 16),), jnp.float32)
    offset_init = centred(key_list[5], (NOFF, NF), 1.0, 6.0, (), jnp.float32)
    return {"traces": traces, "source_ids": source_ids, "receiver_ids": receiver_ids, "offset_ids": offset_ids, "receiver_init": receiver_init, "offset_init": offset_init}


def dft_tables(samples, start, count):
    times = jnp.arange(samples, dtype=jnp.int32)[:, None]
    bins = (start + jnp.arange(count, dtype=jnp.int32))[None, :]
    phase = (times * bins) % samples
    angle = phase.astype(jnp.float32) * (2.0 * 3.141592653589793 / samples)
    return jnp.concatenate([jnp.cos(angle), -jnp.sin(angle)], axis=1).astype(jnp.bfloat16)


def log_spectra(block, tables, count):
    both = jnp.dot(block, tables, preferred_element_type=jnp.float32)
    real = both[:, :count]
    imag = both[:, count:]
    power = (real * real + imag * imag) / block.shape[1]
    return 0.5 * jnp.log(power + 0.25)


def reference(traces, source_ids, receiver_ids, offset_ids, receiver_init, offset_init):
    blocks_s, blocks_r, per_dev, samples = traces.shape
    bins = receiver_init.shape[1]
    tables = dft_tables(samples, 0, bins)
    flat = traces.reshape(blocks_s * blocks_r, per_dev, samples)
    spectra = lax.map(lambda block: log_spectra(block, tables, bins), flat)
    spectra = spectra.reshape(blocks_s * blocks_r * per_dev, bins)
    src_base = jnp.arange(blocks_s, dtype=jnp.int32)[:, None, None] * NSRC_DEV
    rcv_base = jnp.arange(blocks_r, dtype=jnp.int32)[None, :, None] * NRCV_DEV
    src_glob = (source_ids + src_base).reshape(-1).astype(jnp.int32)
    rcv_glob = (receiver_ids + rcv_base).reshape(-1).astype(jnp.int32)
    off_glob = offset_ids.reshape(-1).astype(jnp.int32)
    n_src = NSRC_DEV * blocks_s
    n_rcv = NRCV_DEV * blocks_r
    n_off = offset_init.shape[0]
    ones = jnp.ones(src_glob.shape, jnp.float32)
    src_count = jax.ops.segment_sum(ones, src_glob, num_segments=n_src)
    rcv_count = jax.ops.segment_sum(ones, rcv_glob, num_segments=n_rcv)
    off_count = jax.ops.segment_sum(ones, off_glob, num_segments=n_off)
    base = spectra - receiver_init[rcv_glob] - offset_init[off_glob]
    source_terms = jax.ops.segment_sum(base, src_glob, num_segments=n_src) / (src_count + 1.0)[:, None]
    after = spectra - source_terms[src_glob] - offset_init[off_glob]
    receiver_terms = jax.ops.segment_sum(after, rcv_glob, num_segments=n_rcv) / (rcv_count + 1.0)[:, None]
    later = spectra - source_terms[src_glob] - receiver_terms[rcv_glob]
    offset_terms = jax.ops.segment_sum(later, off_glob, num_segments=n_off) / (off_count + 1.0)[:, None]
    residual = later - offset_terms[off_glob]
    return source_terms, receiver_terms, offset_terms, residual.reshape(blocks_s, blocks_r, per_dev, bins)
```

```python
import functools

import jax
import jax.numpy as jnp
import ml_dtypes
import numpy as np
from jax import lax
from jax.experimental import pallas as pl
from jax.experimental.pallas import tpu as pltpu
from jax.sharding import PartitionSpec as P

NSRC = 32
NRCV = 32
NOFF = 64
ROWS = NSRC + NRCV + NOFF
MESH = pl.DeviceIdType.MESH
HIGHEST = lax.Precision.HIGHEST


def dft_tables(samples, bins, chunks):
    times = np.arange(samples, dtype=np.int64)[:, None]
    freqs = np.arange(bins, dtype=np.int64)[None, :]
    phase = (times * freqs) % samples
    angle = phase.astype(np.float32) * np.float32(2.0 * 3.141592653589793 / samples)
    cosine = np.cos(angle).astype(ml_dtypes.bfloat16)
    sine = (-np.sin(angle)).astype(ml_dtypes.bfloat16)
    width = bins // chunks
    return np.stack(
        [
            np.concatenate([t[:, c * width : (c + 1) * width] for t in (cosine, sine)], axis=1)
            for c in range(chunks)
        ]
    )


def hot_rows(src, rcv, off):
    parts = []
    for ids, count in ((src, NSRC), (rcv, NRCV), (off, NOFF)):
        rows = lax.broadcasted_iota(jnp.int32, (count, ids.shape[1]), 0)
        parts.append((rows == ids).astype(jnp.float32))
    return jnp.concatenate(parts, axis=0)


def split(values):
    high = values.astype(jnp.bfloat16)
    low = (values - high.astype(jnp.float32)).astype(jnp.bfloat16)
    return high, low


def dot(a, b):
    return jnp.dot(a, b, preferred_element_type=jnp.float32)


def local_kernel(
    samples, traces_ref, tables_ref, src_ref, rcv_ref, off_ref, rinit_ref, oinit_ref,
    spectra_ref, sums_ref, gram_ref,
):
    width = spectra_ref.shape[1]
    both = dot(traces_ref[...], tables_ref[0])
    real, imag = both[:, :width], both[:, width:]
    spectra = 0.5 * jnp.log((real * real + imag * imag) * (1.0 / samples) + 0.25)
    spectra_ref[...] = spectra

    hot = hot_rows(src_ref[...], rcv_ref[...], off_ref[...]).astype(jnp.bfloat16)
    gram = lax.dot_general(hot, hot, (((1,), (1,)), ((), ())), preferred_element_type=jnp.float32)
    gram_ref[...] = gram
    row = lax.broadcasted_iota(jnp.int32, (ROWS, ROWS), 0)
    lane = lax.broadcasted_iota(jnp.int32, (ROWS, ROWS), 1)
    from_rcv = (lane >= NSRC) & (lane < NSRC + NRCV) & (row < NSRC)
    from_off = (lane >= NSRC + NRCV) & (row < NSRC + NRCV)
    before = jnp.where(from_rcv | from_off, gram, 0.0).astype(jnp.bfloat16)
    zeros = jnp.zeros((NSRC, width), jnp.float32)
    init = jnp.concatenate([zeros, rinit_ref[...], oinit_ref[...]], axis=0)
    spec_high, spec_low = split(spectra)
    init_high, init_low = split(init)
    sums = (dot(hot, spec_high) - dot(before, init_high)) + (dot(hot, spec_low) - dot(before, init_low))
    turned = sums.T
    slices, rows, _ = sums_ref.shape
    per = rows - NSRC
    for k in range(slices):
        sums_ref[k, :per, :] = turned[k * per : (k + 1) * per]
        sums_ref[k, per:, :] = gram[:NSRC]


def spectra_and_sums(traces, src, rcv, off, receiver_init, offset_init, parts):
    traces_n, samples = traces.shape
    bins = receiver_init.shape[1]
    chunks = max(1, bins // 256)
    width = bins // chunks
    per = bins // parts
    tables = jnp.asarray(dft_tables(samples, bins, chunks))
    whole = lambda c: (0, 0)
    along = lambda c: (0, c)
    return pl.pallas_call(
        functools.partial(local_kernel, samples),
        grid=(chunks,),
        in_specs=[
            pl.BlockSpec((traces_n, samples), whole),
            pl.BlockSpec((1, samples, 2 * width), lambda c: (c, 0, 0)),
            pl.BlockSpec((1, traces_n), whole),
            pl.BlockSpec((1, traces_n), whole),
            pl.BlockSpec((1, traces_n), whole),
            pl.BlockSpec((NRCV, width), along),
            pl.BlockSpec((NOFF, width), along),
        ],
        out_specs=[
            pl.BlockSpec((traces_n, width), along),
            pl.BlockSpec((parts // chunks, per + NSRC, ROWS), lambda c: (c, 0, 0)),
            pl.BlockSpec((ROWS, ROWS), whole),
        ],
        out_shape=[
            jax.ShapeDtypeStruct((traces_n, bins), jnp.float32),
            jax.ShapeDtypeStruct((parts, per + NSRC, ROWS), jnp.float32),
            jax.ShapeDtypeStruct((ROWS, ROWS), jnp.float32),
        ],
        compiler_params=pltpu.CompilerParams(
            dimension_semantics=("arbitrary",), vmem_limit_bytes=32 * 1024 * 1024
        ),
    )(traces, tables, src, rcv, off, receiver_init, offset_init)


def pick(tiles, lane):
    out = pltpu.roll(tiles[0], ROWS - 32, 1)
    out = jnp.where(lane < 32, out, tiles[1])
    out = jnp.where(lane < 64, out, pltpu.roll(tiles[2], 32, 1))
    return jnp.where(lane < 96, out, pltpu.roll(tiles[3], 64, 1))


def sweep_kernel(
    nj, ny, nz, sums_ref, gram_ref, terms_ref,
    a_buf, gy_buf, gz_buf, gr_buf, p_buf, b1_buf, b2_buf, c_buf, d_out, d_buf,
    a_send, a_recv, gy_send, gy_recv, gz_send, gz_recv, gr_send, gr_recv,
    b1_send, b1_recv, b2_send, b2_recv, c_send, c_recv, d_send, d_recv,
):
    i = lax.axis_index("src")
    j = lax.axis_index("rcv")
    y = i // nz
    z = i % nz
    per = a_buf.shape[1] - NSRC
    tiles = nj * NRCV // ROWS

    def over_j(d):
        peer = (j + d) % nj
        return peer, (i, peer)

    def over_y(d):
        peer = (y + d) % ny
        return peer, (peer * nz + z, j)

    def over_z(d):
        peer = (z + d) % nz
        return peer, (y * nz + peer, j)

    def loop(n, body):
        def step(d, carry):
            body(d)
            return carry

        lax.fori_loop(1, n, step, 0)

    def send(n, over, me, source, buf, send_sem, recv_sem):
        def body(d):
            peer, device = over(d)
            pltpu.make_async_remote_copy(
                src_ref=source(peer), dst_ref=buf.at[me], send_sem=send_sem.at[d],
                recv_sem=recv_sem.at[me], device_id=device, device_id_type=MESH,
            ).start()

        loop(n, body)

    def arrive(n, over, buf, send_sem, recv_sem):
        def body(d):
            peer, device = over(d)
            pltpu.make_async_remote_copy(
                src_ref=buf.at[peer], dst_ref=buf.at[peer], send_sem=send_sem.at[d],
                recv_sem=recv_sem.at[peer], device_id=device, device_id_type=MESH,
            ).wait_recv()

        loop(n, body)

    def sent(n, over, me, source, buf, send_sem, recv_sem):
        def body(d):
            peer, device = over(d)
            pltpu.make_async_remote_copy(
                src_ref=source(peer), dst_ref=buf.at[me], send_sem=send_sem.at[d],
                recv_sem=recv_sem.at[me], device_id=device, device_id_type=MESH,
            ).wait_send()

        loop(n, body)

    barrier = pltpu.get_barrier_semaphore()
    for n, over in ((nj, over_j), (ny, over_y), (nz, over_z)):
        def greet(d, over=over):
            pl.semaphore_signal(barrier, inc=1, device_id=over(d)[1], device_id_type=MESH)

        loop(n, greet)
    pl.semaphore_wait(barrier, nj + ny + nz - 3)

    count_y = (ny, over_y, y, lambda p: gy_buf.at[y], gy_buf, gy_send, gy_recv)
    gy_buf[y] = gram_ref[NSRC : NSRC + NRCV, :]
    send(*count_y)
    sums_j = (nj, over_j, j, lambda p: sums_ref.at[p], a_buf, a_send, a_recv)
    send(*sums_j)
    a_buf[j] = sums_ref[j]

    count_z = (nz, over_z, z, lambda p: gz_buf.at[z], gz_buf, gz_send, gz_recv)
    arrive(ny, over_y, gy_buf, gy_send, gy_recv)
    gz_buf[z] = jnp.sum(gy_buf[...], axis=0)
    send(*count_z)

    arrive(nj, over_j, a_buf, a_send, a_recv)
    total = jnp.sum(a_buf[...], axis=0)
    lane = lax.broadcasted_iota(jnp.int32, (per, ROWS), 1)
    n_src = jnp.sum(total[per:], axis=0, keepdims=True)
    src_terms = jnp.where(lane < NSRC, total[:per] / (n_src + 1.0), 0.0)
    counts = jnp.concatenate([a_buf[q, per:, :] for q in range(nj)], axis=1)
    along = jnp.dot(
        src_terms[:, :NSRC], counts, precision=HIGHEST, preferred_element_type=jnp.float32
    )
    left = [a_buf[q, :per, :] - along[:, q * ROWS : (q + 1) * ROWS] for q in range(nj)]
    packed = [pick(left[4 * t : 4 * t + 4], lane) for t in range(tiles)]
    packed.append(functools.reduce(lambda a, b: a + b, left))
    few = per // ny
    for t in range(tiles + 1):
        p_buf[:, :, t * ROWS : (t + 1) * ROWS] = packed[t].reshape(ny, few, ROWS)
    part_y = (ny, over_y, y, lambda p: p_buf.at[p], b1_buf, b1_send, b1_recv)
    send(*part_y)
    b1_buf[y] = p_buf[y]

    count_j = (nj, over_j, j, lambda p: gr_buf.at[j], gr_buf, gr_send, gr_recv)
    arrive(nz, over_z, gz_buf, gz_send, gz_recv)
    gr_buf[j] = jnp.sum(gz_buf[...], axis=0)
    send(*count_j)

    part_z = (nz, over_z, z, lambda p: b2_buf.at[z], b2_buf, b2_send, b2_recv)
    arrive(ny, over_y, b1_buf, b1_send, b1_recv)
    b2_buf[z] = jnp.sum(b1_buf[...], axis=0)
    send(*part_z)

    arrive(nj, over_j, gr_buf, gr_send, gr_recv)
    by_rcv = gr_buf[...]
    columns = [jnp.sum(by_rcv[q], axis=0, keepdims=True) for q in range(nj)]
    n_off = functools.reduce(lambda a, b: a + b, columns)
    n_rcv = [
        pick([jnp.broadcast_to(c, (few, ROWS)) for c in columns[4 * t : 4 * t + 4]], lane[:few])
        for t in range(tiles)
    ]
    n_rcv = jnp.concatenate(n_rcv, axis=1)
    arrive(nz, over_z, b2_buf, b2_send, b2_recv)
    reduced = b2_buf[0]
    for q in range(1, nz):
        reduced = reduced + b2_buf[q]
    rcv_terms = reduced[:, : tiles * ROWS] / (n_rcv + 1.0)
    later = reduced[:, tiles * ROWS :] - jnp.dot(
        rcv_terms, by_rcv.reshape(nj * NRCV, ROWS), precision=HIGHEST,
        preferred_element_type=jnp.float32,
    )
    off_terms = later / (n_off + 1.0)
    c_buf[y] = jnp.concatenate([rcv_terms, off_terms], axis=1)
    terms_y = (ny, over_y, y, lambda p: c_buf.at[y], c_buf, c_send, c_recv)
    send(*terms_y)
    arrive(ny, over_y, c_buf, c_send, c_recv)

    off_tile = c_buf[:, :, tiles * ROWS :].reshape(per, ROWS)
    for t in range(tiles):
        tile = c_buf[:, :, t * ROWS : (t + 1) * ROWS].reshape(per, ROWS)
        for q in range(4):
            turned = tile if q == 1 else pltpu.roll(tile, (32 - 32 * q) % ROWS, 1)
            d_out[4 * t + q] = jnp.where(
                lane < NSRC, src_terms, jnp.where(lane < NSRC + NRCV, turned, off_tile)
            )
    back_j = (nj, over_j, j, lambda p: d_out.at[p], d_buf, d_send, d_recv)
    send(*back_j)
    d_buf[j] = d_out[j]
    arrive(nj, over_j, d_buf, d_send, d_recv)
    terms_ref[...] = d_buf[...].reshape(nj * per, ROWS).T

    for copies in (count_y, sums_j, count_z, part_y, count_j, part_z, terms_y, back_j):
        sent(*copies)


def sweep(sums, gram, nj, ny, nz):
    per = sums.shape[1] - NSRC
    bins = nj * per
    few = per // ny
    wide = nj * NRCV + ROWS
    vmem = pl.BlockSpec(memory_space=pltpu.VMEM)
    f32 = jnp.float32
    dma = lambda n: [pltpu.SemaphoreType.DMA((n,)), pltpu.SemaphoreType.DMA((n,))]
    return pl.pallas_call(
        functools.partial(sweep_kernel, nj, ny, nz),
        in_specs=[vmem, vmem],
        out_specs=vmem,
        out_shape=jax.ShapeDtypeStruct((ROWS, bins), f32),
        scratch_shapes=[
            pltpu.VMEM((nj, per + NSRC, ROWS), f32),
            pltpu.VMEM((ny, NRCV, ROWS), f32),
            pltpu.VMEM((nz, NRCV, ROWS), f32),
            pltpu.VMEM((nj, NRCV, ROWS), f32),
            pltpu.VMEM((ny, few, wide), f32),
            pltpu.VMEM((ny, few, wide), f32),
            pltpu.VMEM((nz, few, wide), f32),
            pltpu.VMEM((ny, few, wide), f32),
            pltpu.VMEM((nj, per, ROWS), f32),
            pltpu.VMEM((nj, per, ROWS), f32),
            *dma(nj), *dma(ny), *dma(nz), *dma(nj), *dma(ny), *dma(nz), *dma(ny), *dma(nj),
        ],
        compiler_params=pltpu.CompilerParams(
            collective_id=0, has_side_effects=True, vmem_limit_bytes=32 * 1024 * 1024
        ),
    )(sums, gram)


def on_device(
    nj, ny, nz, traces, source_ids, receiver_ids, offset_ids, receiver_init, offset_init
):
    src, rcv, off = source_ids[0], receiver_ids[0], offset_ids[0]
    spectra, sums, gram = spectra_and_sums(
        traces[0, 0], src, rcv, off, receiver_init, offset_init, nj
    )
    terms = sweep(sums, gram, nj, ny, nz)
    hot = hot_rows(src, rcv, off)
    residual = spectra - jnp.dot(
        hot.T, terms, precision=HIGHEST, preferred_element_type=jnp.float32
    )
    return (
        terms[:NSRC], terms[NSRC : NSRC + NRCV], terms[NSRC + NRCV :], residual[None, None]
    )


def solution(mesh):
    nsrc, nj = mesh.shape["src"], mesh.shape["rcv"]
    nz = 4 if nsrc >= 32 else 2
    ny = nsrc // nz
    placed = (
        P("src", "rcv", None, None),
        P("src", "rcv", None),
        P("src", "rcv", None),
        P("src", "rcv", None),
        P("rcv", None),
        P(),
    )
    return jax.shard_map(
        functools.partial(on_device, nj, ny, nz),
        mesh=mesh,
        in_specs=placed,
        out_specs=(P("src", None), P("rcv", None), P(), P("src", "rcv", None, None)),
        check_vma=False,
    )
```

```python
import functools

import jax
import jax.numpy as jnp
import ml_dtypes
import numpy as np
from jax import lax
from jax.experimental import pallas as pl
from jax.experimental.pallas import tpu as pltpu
from jax.sharding import PartitionSpec as P

NSRC = 32
NRCV = 32
NOFF = 64
ROWS = NSRC + NRCV + NOFF
MESH = pl.DeviceIdType.MESH
HIGHEST = lax.Precision.HIGHEST


def dft_tables(samples, bins, chunks):
    times = np.arange(samples, dtype=np.int64)[:, None]
    freqs = np.arange(bins, dtype=np.int64)[None, :]
    phase = (times * freqs) % samples
    angle = phase.astype(np.float32) * np.float32(2.0 * 3.141592653589793 / samples)
    cosine = np.cos(angle).astype(ml_dtypes.bfloat16)
    sine = (-np.sin(angle)).astype(ml_dtypes.bfloat16)
    width = bins // chunks
    return np.stack(
        [
            np.concatenate([t[:, c * width : (c + 1) * width] for t in (cosine, sine)], axis=1)
            for c in range(chunks)
        ]
    )


def hot_rows(src, rcv, off):
    parts = []
    for ids, count in ((src, NSRC), (rcv, NRCV), (off, NOFF)):
        rows = lax.broadcasted_iota(jnp.int32, (count, ids.shape[1]), 0)
        parts.append((rows == ids).astype(jnp.float32))
    return jnp.concatenate(parts, axis=0)


def split(values):
    high = values.astype(jnp.bfloat16)
    low = (values - high.astype(jnp.float32)).astype(jnp.bfloat16)
    return high, low


def dot(a, b):
    return jnp.dot(a, b, preferred_element_type=jnp.float32)


def tiles_of(values, count):
    return [values[:, t * ROWS : (t + 1) * ROWS] for t in range(count)]


def pick(tiles, lane):
    out = pltpu.roll(tiles[0], ROWS - 32, 1)
    out = jnp.where(lane < 32, out, tiles[1])
    out = jnp.where(lane < 64, out, pltpu.roll(tiles[2], 32, 1))
    return jnp.where(lane < 96, out, pltpu.roll(tiles[3], 64, 1))


def sweep_kernel(
    nj, ny, nz, chunks,
    traces_hbm, tables_hbm, src_hbm, rcv_hbm, off_hbm, rinit_hbm, oinit_hbm,
    spectra_hbm, terms_ref, hot_ref,
    traces_buf, tables_buf, ids_buf, init_buf, x_buf, sums_buf,
    gy_buf, gs_buf, gz_buf, gr_buf, a_buf, p_buf, b1_buf, b2_buf, c_buf, d_out, d_buf,
    load_sem, table_sem, store_sem, send_sem, recv_sem,
):
    i = lax.axis_index("src")
    j = lax.axis_index("rcv")
    y = i // nz
    z = lax.rem(i, nz)
    samples = traces_buf.shape[1]
    width = x_buf.shape[2]
    per = a_buf.shape[1]
    few = per // ny
    tiles = nj * NRCV // ROWS
    each = nj // chunks
    first = j // each

    loads = [
        pltpu.make_async_copy(src_hbm, ids_buf.at[0], load_sem.at[0]),
        pltpu.make_async_copy(rcv_hbm, ids_buf.at[1], load_sem.at[1]),
        pltpu.make_async_copy(off_hbm, ids_buf.at[2], load_sem.at[2]),
        pltpu.make_async_copy(traces_hbm, traces_buf, load_sem.at[3]),
        pltpu.make_async_copy(rinit_hbm, init_buf.at[pl.ds(0, NRCV)], load_sem.at[4]),
        pltpu.make_async_copy(oinit_hbm, init_buf.at[pl.ds(NRCV, NOFF)], load_sem.at[5]),
    ]
    order = [lax.rem(first + k, chunks) for k in range(chunks)]
    tables = [
        pltpu.make_async_copy(tables_hbm.at[c], tables_buf.at[c], table_sem.at[k])
        for k, c in enumerate(order)
    ]
    for copy in loads[:4] + tables[:1] + loads[4:] + tables[1:]:
        copy.start()

    def over_j(d):
        peer = lax.rem(j + d, nj)
        return peer, (i, peer)

    def over_y(d):
        peer = lax.rem(y + d, ny)
        return peer, (peer * nz + z, j)

    def over_z(d):
        peer = lax.rem(z + d, nz)
        return peer, (y * nz + peer, j)

    def copy_to(device, source, target, phase):
        return pltpu.make_async_remote_copy(
            src_ref=source, dst_ref=target, send_sem=send_sem.at[phase],
            recv_sem=recv_sem.at[phase], device_id=device, device_id_type=MESH,
        )

    def send(n, over, me, source, buf, phase):
        for d in range(1, n):
            peer, device = over(d)
            copy_to(device, source(peer), buf.at[me], phase).start()

    def all_of(n, over, buf, phase):
        part = buf.at[pl.ds(0, n - 1)]
        return copy_to(over(1)[1], part, part, phase)

    barrier = pltpu.get_barrier_semaphore()
    for n, over in ((ny, over_y), (nj, over_j), (nz, over_z)):
        for d in range(1, n):
            pl.semaphore_signal(barrier, inc=1, device_id=over(d)[1], device_id_type=MESH)

    for copy in loads[:3]:
        copy.wait()
    hot = hot_rows(ids_buf[0], ids_buf[1], ids_buf[2])
    hot_ref[...] = hot.T.astype(jnp.bfloat16)
    hot = hot.astype(jnp.bfloat16)
    gram = lax.dot_general(hot, hot, (((1,), (1,)), ((), ())), preferred_element_type=jnp.float32)
    gy_buf[y] = gram[NSRC : NSRC + NRCV]
    gs_buf[j] = gram[:NSRC]
    row = lax.broadcasted_iota(jnp.int32, (ROWS, ROWS), 0)
    lane = lax.broadcasted_iota(jnp.int32, (ROWS, ROWS), 1)
    from_rcv = (lane >= NSRC) & (lane < NSRC + NRCV) & (row < NSRC)
    from_off = (lane >= NSRC + NRCV) & (row < NSRC + NRCV)
    before = jnp.where(from_rcv | from_off, gram, 0.0).astype(jnp.bfloat16)[:, NSRC:]
    pl.semaphore_wait(barrier, nj + ny + nz - 3)
    send(ny, over_y, y, lambda p: gy_buf.at[y], gy_buf, 0)
    send(nj, over_j, j, lambda p: gs_buf.at[j], gs_buf, 1)

    for copy in loads[3:]:
        copy.wait()
    stores = []
    for k, c in enumerate(order):
        tables[k].wait()
        both = dot(traces_buf[...], tables_buf[c])
        real, imag = both[:, :width], both[:, width:]
        spectra = 0.5 * jnp.log((real * real + imag * imag) * (1.0 / samples) + 0.25)
        x_buf[c] = spectra
        store = pltpu.make_async_copy(x_buf.at[c], spectra_hbm.at[c], store_sem.at[k])
        store.start()
        stores.append(store)
        init = init_buf[:, pl.ds(pl.multiple_of(c * width, width), width)]
        spec_high, spec_low = split(spectra)
        init_high, init_low = split(init)
        sums = (dot(hot, spec_high) - dot(before, init_high)) + (
            dot(hot, spec_low) - dot(before, init_low)
        )
        turned = sums.T
        for q in range(each):
            sums_buf[c * each + q] = turned[q * per : (q + 1) * per]
        for q in range(1 if k == 0 else 0, each):
            peer = c * each + (lax.rem(j + q, each) if k == 0 else q)
            copy_to((i, peer), sums_buf.at[peer], a_buf.at[j], 2).start()
    a_buf[j] = sums_buf[j]

    all_of(ny, over_y, gy_buf, 0).wait_recv()
    gz_buf[z] = jnp.sum(gy_buf[...], axis=0)
    send(nz, over_z, z, lambda p: gz_buf.at[z], gz_buf, 3)
    all_of(nj, over_j, gs_buf, 1).wait_recv()
    lane = lax.broadcasted_iota(jnp.int32, (per, ROWS), 1)
    by_src = [gs_buf[q] for q in range(nj)]
    src_count = functools.reduce(lambda a, b: a + b, by_src)
    n_src = jnp.sum(src_count, axis=0, keepdims=True) + 1.0
    off_high, off_low = split(src_count)
    counts = [
        pick(by_src[4 * t : 4 * t + 4], lane[:NSRC]).astype(jnp.bfloat16) for t in range(tiles)
    ]
    counts = jnp.concatenate(counts + [off_high, off_low], axis=1)
    all_of(nz, over_z, gz_buf, 3).wait_recv()
    gr_buf[j] = jnp.sum(gz_buf[...], axis=0)
    send(nj, over_j, j, lambda p: gr_buf.at[j], gr_buf, 4)

    all_of(nj, over_j, a_buf, 2).wait_recv()
    parts = [a_buf[q] for q in range(nj)]
    total = functools.reduce(lambda a, b: a + b, parts)
    src_terms = jnp.where(lane < NSRC, total / n_src, 0.0)
    both = dot(jnp.concatenate(split(src_terms[:, :NSRC]), axis=0), counts)
    along = tiles_of(both[:per] + both[per:], tiles + 2)
    for t in range(tiles):
        left = pick(parts[4 * t : 4 * t + 4], lane) - along[t]
        p_buf[:, :, t * ROWS : (t + 1) * ROWS] = left.reshape(ny, few, ROWS)
    left = total - along[tiles] - along[tiles + 1]
    p_buf[:, :, tiles * ROWS :] = left.reshape(ny, few, ROWS)
    send(ny, over_y, y, lambda p: p_buf.at[p], b1_buf, 5)
    b1_buf[y] = p_buf[y]

    all_of(nj, over_j, gr_buf, 4).wait_recv()
    by_rcv = gr_buf[...]
    columns = [jnp.sum(by_rcv[q], axis=0, keepdims=True) for q in range(nj)]
    n_off = functools.reduce(lambda a, b: a + b, columns) + 1.0
    columns = [jnp.broadcast_to(c, (few, ROWS)) for c in columns]
    n_rcv = [pick(columns[4 * t : 4 * t + 4], lane[:few]) for t in range(tiles)]
    n_rcv = jnp.concatenate(n_rcv, axis=1) + 1.0
    by_rcv = jnp.concatenate(split(by_rcv.reshape(nj * NRCV, ROWS)), axis=1)

    all_of(ny, over_y, b1_buf, 5).wait_recv()
    b2_buf[z] = jnp.sum(b1_buf[...], axis=0)
    send(nz, over_z, z, lambda p: b2_buf.at[z], b2_buf, 6)
    all_of(nz, over_z, b2_buf, 6).wait_recv()

    reduced = b2_buf[0]
    for q in range(1, nz):
        reduced = reduced + b2_buf[q]
    rcv_terms = reduced[:, : tiles * ROWS] / n_rcv
    both = dot(jnp.concatenate(split(rcv_terms), axis=0), by_rcv)
    both = both[:few] + both[few:]
    later = reduced[:, tiles * ROWS :] - both[:, :ROWS] - both[:, ROWS:]
    c_buf[y] = jnp.concatenate([rcv_terms, later / n_off], axis=1)
    send(ny, over_y, y, lambda p: c_buf.at[y], c_buf, 7)
    all_of(ny, over_y, c_buf, 7).wait_recv()

    off_tile = c_buf[:, :, tiles * ROWS :].reshape(per, ROWS)
    for t in range(tiles):
        tile = c_buf[:, :, t * ROWS : (t + 1) * ROWS].reshape(per, ROWS)
        for q in range(4):
            turned = tile if q == 1 else pltpu.roll(tile, (32 - 32 * q) % ROWS, 1)
            d_out[4 * t + q] = jnp.where(
                lane < NSRC, src_terms, jnp.where(lane < NSRC + NRCV, turned, off_tile)
            )
    send(nj, over_j, j, lambda p: d_out.at[p], d_buf, 8)
    d_buf[j] = d_out[j]
    for phase, (n, over, buf) in enumerate((
        (ny, over_y, gy_buf), (nj, over_j, gs_buf), (nj, over_j, a_buf), (nz, over_z, gz_buf),
        (nj, over_j, gr_buf), (ny, over_y, b1_buf), (nz, over_z, b2_buf), (ny, over_y, c_buf),
        (nj, over_j, d_buf),
    )):
        all_of(n, over, buf, phase).wait_send()
    for store in stores:
        store.wait()
    all_of(nj, over_j, d_buf, 8).wait_recv()
    terms_ref[...] = d_buf[...].reshape(nj * per, ROWS)


def sweep(traces, src, rcv, off, receiver_init, offset_init, nj, ny, nz):
    traces_n, samples = traces.shape
    bins = receiver_init.shape[1]
    chunks = max(1, bins // 256)
    width = bins // chunks
    per = bins // nj
    few = per // ny
    wide = nj * NRCV + ROWS
    f32, b16 = jnp.float32, jnp.bfloat16
    tables = jnp.asarray(dft_tables(samples, bins, chunks))
    hbm = pl.BlockSpec(memory_space=pltpu.HBM)
    dma = pltpu.SemaphoreType.DMA
    return pl.pallas_call(
        functools.partial(sweep_kernel, nj, ny, nz, chunks),
        in_specs=[hbm] * 7,
        out_specs=[pl.BlockSpec(memory_space=pl.ANY)] + [pl.BlockSpec(memory_space=pltpu.VMEM)] * 2,
        out_shape=[
            jax.ShapeDtypeStruct((chunks, traces_n, width), f32),
            jax.ShapeDtypeStruct((bins, ROWS), f32),
            jax.ShapeDtypeStruct((traces_n, ROWS), b16),
        ],
        scratch_shapes=[
            pltpu.VMEM((traces_n, samples), b16),
            pltpu.VMEM((chunks, samples, 2 * width), b16),
            pltpu.VMEM((3, 1, traces_n), jnp.int32),
            pltpu.VMEM((NRCV + NOFF, bins), f32),
            pltpu.VMEM((chunks, traces_n, width), f32),
            pltpu.VMEM((nj, per, ROWS), f32),
            pltpu.VMEM((ny, NRCV, ROWS), f32),
            pltpu.VMEM((nj, NSRC, ROWS), f32),
            pltpu.VMEM((nz, NRCV, ROWS), f32),
            pltpu.VMEM((nj, NRCV, ROWS), f32),
            pltpu.VMEM((nj, per, ROWS), f32),
            pltpu.VMEM((ny, few, wide), f32),
            pltpu.VMEM((ny, few, wide), f32),
            pltpu.VMEM((nz, few, wide), f32),
            pltpu.VMEM((ny, few, wide), f32),
            pltpu.VMEM((nj, per, ROWS), f32),
            pltpu.VMEM((nj, per, ROWS), f32),
            dma((6,)), dma((chunks,)), dma((chunks,)), dma((9,)), dma((9,)),
        ],
        compiler_params=pltpu.CompilerParams(
            collective_id=0, has_side_effects=True, vmem_limit_bytes=60 * 1024 * 1024
        ),
    )(traces, tables, src, rcv, off, receiver_init, offset_init)


def finish_kernel(
    hot_ref, spectra_ref, turned_ref, src_out, rcv_out, off_out, residual_ref
):
    hot = hot_ref[...]
    turned = turned_ref[...]
    high, low = split(turned)
    over_lanes = (((1,), (1,)), ((), ()))
    spread = lax.dot_general(hot, high, over_lanes, preferred_element_type=jnp.float32)
    spread += lax.dot_general(hot, low, over_lanes, preferred_element_type=jnp.float32)
    residual_ref[0, 0] = spectra_ref[0] - spread
    terms = turned.T
    src_out[...] = terms[:NSRC]
    rcv_out[...] = terms[NSRC : NSRC + NRCV]
    off_out[...] = terms[NSRC + NRCV :]


def finish(hot, spectra, turned):
    chunks, traces_n, width = spectra.shape
    bins = chunks * width
    whole = lambda c: (0, 0)
    along = lambda c: (0, c)
    f32 = jnp.float32
    return pl.pallas_call(
        finish_kernel,
        grid=(chunks,),
        in_specs=[
            pl.BlockSpec((traces_n, ROWS), whole),
            pl.BlockSpec((1, traces_n, width), lambda c: (c, 0, 0)),
            pl.BlockSpec((width, ROWS), lambda c: (c, 0)),
        ],
        out_specs=[
            pl.BlockSpec((NSRC, width), along),
            pl.BlockSpec((NRCV, width), along),
            pl.BlockSpec((NOFF, width), along),
            pl.BlockSpec((1, 1, traces_n, width), lambda c: (0, 0, 0, c)),
        ],
        out_shape=[
            jax.ShapeDtypeStruct((NSRC, bins), f32),
            jax.ShapeDtypeStruct((NRCV, bins), f32),
            jax.ShapeDtypeStruct((NOFF, bins), f32),
            jax.ShapeDtypeStruct((1, 1, traces_n, bins), f32),
        ],
        compiler_params=pltpu.CompilerParams(
            dimension_semantics=("arbitrary",), vmem_limit_bytes=60 * 1024 * 1024
        ),
    )(hot, spectra, turned)


def on_device(
    nj, ny, nz, traces, source_ids, receiver_ids, offset_ids, receiver_init, offset_init
):
    src, rcv, off = source_ids[0], receiver_ids[0], offset_ids[0]
    spectra, turned, hot = sweep(
        traces[0, 0], src, rcv, off, receiver_init, offset_init, nj, ny, nz
    )
    return finish(hot, spectra, turned)


def solution(mesh):
    nsrc, nj = mesh.shape["src"], mesh.shape["rcv"]
    nz = 4 if nsrc >= 32 else 2
    ny = nsrc // nz
    placed = (
        P("src", "rcv", None, None),
        P("src", "rcv", None),
        P("src", "rcv", None),
        P("src", "rcv", None),
        P("rcv", None),
        P(),
    )
    return jax.shard_map(
        functools.partial(on_device, nj, ny, nz),
        mesh=mesh,
        in_specs=placed,
        out_specs=(P("src", None), P("rcv", None), P(), P("src", "rcv", None, None)),
        check_vma=False,
    )
```

```python
import functools

import jax
import jax.numpy as jnp
import ml_dtypes
import numpy as np
from jax import lax
from jax.experimental import pallas as pl
from jax.experimental.pallas import tpu as pltpu
from jax.sharding import PartitionSpec as P

NSRC = 32
NRCV = 32
NOFF = 64
ROWS = NSRC + NRCV + NOFF
MESH = pl.DeviceIdType.MESH
OVER_LANES = (((1,), (1,)), ((), ()))


def dft_tables(samples, bins, chunks):
    times = np.arange(samples, dtype=np.int64)[:, None]
    freqs = np.arange(bins, dtype=np.int64)[None, :]
    phase = (times * freqs) % samples
    angle = phase.astype(np.float32) * np.float32(2.0 * 3.141592653589793 / samples)
    cosine = np.cos(angle).astype(ml_dtypes.bfloat16)
    sine = (-np.sin(angle)).astype(ml_dtypes.bfloat16)
    width = bins // chunks
    return np.stack(
        [
            np.concatenate([t[:, c * width : (c + 1) * width] for t in (cosine, sine)], axis=1)
            for c in range(chunks)
        ]
    )


def hot_rows(src, rcv, off):
    parts = []
    for ids, count in ((src, NSRC), (rcv, NRCV), (off, NOFF)):
        rows = lax.broadcasted_iota(jnp.int32, (count, ids.shape[1]), 0)
        parts.append((rows == ids).astype(jnp.float32))
    return jnp.concatenate(parts, axis=0)


def split(values):
    high = values.astype(jnp.bfloat16)
    low = (values - high.astype(jnp.float32)).astype(jnp.bfloat16)
    return high, low


def dot(a, b):
    return jnp.dot(a, b, preferred_element_type=jnp.float32)


def tiles_of(values, count):
    return [values[:, t * ROWS : (t + 1) * ROWS] for t in range(count)]


def pick(tiles, lane):
    out = pltpu.roll(tiles[0], ROWS - 32, 1)
    out = jnp.where(lane < 32, out, tiles[1])
    out = jnp.where(lane < 64, out, pltpu.roll(tiles[2], 32, 1))
    return jnp.where(lane < 96, out, pltpu.roll(tiles[3], 64, 1))


HALVES = 2


def add(values):
    return functools.reduce(lambda a, b: a + b, values)


def sweep_kernel(
    nj, ny, nz, groups,
    traces_hbm, tables_hbm, src_hbm, rcv_hbm, off_hbm, rinit_hbm, oinit_hbm,
    spectra_hbm, terms_hbm, hot_hbm,
    traces_buf, tables_buf, ids_buf, init_buf, x_buf, hot_buf, sums_buf,
    gy_buf, gz_buf, gr_buf, a_buf, flat_buf, p_buf, b1_buf, b2_buf, c_buf, d_out,
    load_sem, table_sem, store_sem, send_sem, recv_sem,
):
    i = lax.axis_index("src")
    j = lax.axis_index("rcv")
    y = i // nz
    z = lax.rem(i, nz)
    samples = traces_buf.shape[1]
    width = x_buf.shape[2]
    per = a_buf.shape[2]
    few = per // ny
    tiles = nj * NRCV // ROWS
    each = nj // groups
    first = j // each

    mine = ids_buf.at[j]
    loads = [
        pltpu.make_async_copy(src_hbm, mine.at[0], load_sem.at[0]),
        pltpu.make_async_copy(rcv_hbm, mine.at[1], load_sem.at[1]),
        pltpu.make_async_copy(off_hbm, mine.at[2], load_sem.at[2]),
        pltpu.make_async_copy(traces_hbm, traces_buf, load_sem.at[3]),
        pltpu.make_async_copy(rinit_hbm, init_buf.at[pl.ds(0, NRCV)], load_sem.at[4]),
        pltpu.make_async_copy(oinit_hbm, init_buf.at[pl.ds(NRCV, NOFF)], load_sem.at[5]),
    ]
    order = [h * groups + lax.rem(first + k, groups) for h in range(HALVES) for k in range(groups)]
    tables = [
        pltpu.make_async_copy(tables_hbm.at[c], tables_buf.at[c], table_sem.at[k])
        for k, c in enumerate(order)
    ]
    for copy in loads[:4] + tables[:1] + loads[4:] + tables[1:]:
        copy.start()

    def over_j(d):
        peer = lax.rem(j + d, nj)
        return peer, (i, peer)

    def over_y(d):
        peer = lax.rem(y + d, ny)
        return peer, (peer * nz + z, j)

    def over_z(d):
        peer = lax.rem(z + d, nz)
        return peer, (y * nz + peer, j)

    def copy_to(device, source, target, phase):
        return pltpu.make_async_remote_copy(
            src_ref=source, dst_ref=target, send_sem=send_sem.at[phase],
            recv_sem=recv_sem.at[phase], device_id=device, device_id_type=MESH,
        )

    def send(n, over, me, source, buf, phase):
        for d in range(1, n):
            peer, device = over(d)
            copy_to(device, source(peer), buf.at[me], phase).start()

    def all_of(n, over, buf, phase):
        part = buf.at[pl.ds(0, n - 1)]
        return copy_to(over(1)[1], part, part, phase)

    barrier = pltpu.get_barrier_semaphore()
    for n, over in ((ny, over_y), (nj, over_j), (nz, over_z)):
        for d in range(1, n):
            pl.semaphore_signal(barrier, inc=1, device_id=over(d)[1], device_id_type=MESH)

    for copy in loads[:3]:
        copy.wait()
    hot = hot_rows(ids_buf[j, 0], ids_buf[j, 1], ids_buf[j, 2])
    hot_buf[...] = hot.T.astype(jnp.bfloat16)
    hot = hot.astype(jnp.bfloat16)
    gram = lax.dot_general(hot, hot, OVER_LANES, preferred_element_type=jnp.float32)
    gy_buf[y] = gram[NSRC : NSRC + NRCV]
    row = lax.broadcasted_iota(jnp.int32, (ROWS, ROWS), 0)
    lane = lax.broadcasted_iota(jnp.int32, (ROWS, ROWS), 1)
    from_rcv = (lane >= NSRC) & (lane < NSRC + NRCV) & (row < NSRC)
    from_off = (lane >= NSRC + NRCV) & (row < NSRC + NRCV)
    before = jnp.where(from_rcv | from_off, gram, 0.0).astype(jnp.bfloat16)[:, NSRC:]
    pl.semaphore_wait(barrier, nj + ny + nz - 3)
    send(nj, over_j, j, lambda p: ids_buf.at[j], ids_buf, 0)
    send(ny, over_y, y, lambda p: gy_buf.at[y], gy_buf, 1)
    stores = [pltpu.make_async_copy(hot_buf, hot_hbm, load_sem.at[0])]
    stores[0].start()

    for copy in loads[3:]:
        copy.wait()
    for n, c in enumerate(order):
        h, k = n // groups, n % groups
        g = c - h * groups
        tables[n].wait()
        both = dot(traces_buf[...], tables_buf[c])
        real, imag = both[:, :width], both[:, width:]
        spectra = 0.5 * jnp.log((real * real + imag * imag) * (1.0 / samples) + 0.25)
        x_buf[c] = spectra
        store = pltpu.make_async_copy(x_buf.at[c], spectra_hbm.at[c], store_sem.at[n])
        store.start()
        stores.append(store)
        init = init_buf[:, pl.ds(pl.multiple_of(c * width, width), width)]
        spec_high, spec_low = split(spectra)
        init_high, init_low = split(init)
        sums = (dot(hot, spec_high) - dot(before, init_high)) + (
            dot(hot, spec_low) - dot(before, init_low)
        )
        turned = sums.T
        for q in range(each):
            sums_buf[h, g * each + q] = turned[q * per : (q + 1) * per]
        for q in range(1 if k == 0 else 0, each):
            peer = g * each + (lax.rem(j + q, each) if k == 0 else q)
            copy_to((i, peer), sums_buf.at[h, peer], a_buf.at[h, j], 4 + 5 * h).start()
    for h in range(HALVES):
        a_buf[h, j] = sums_buf[h, j]

    all_of(ny, over_y, gy_buf, 1).wait_recv()
    gz_buf[z] = jnp.sum(gy_buf[...], axis=0)
    send(nz, over_z, z, lambda p: gz_buf.at[z], gz_buf, 2)
    all_of(nj, over_j, ids_buf, 0).wait_recv()
    by_src = []
    for q in range(nj):
        peer_hot = hot_rows(ids_buf[q, 0], ids_buf[q, 1], ids_buf[q, 2]).astype(jnp.bfloat16)
        by_src.append(
            lax.dot_general(
                peer_hot[:NSRC], peer_hot, OVER_LANES, preferred_element_type=jnp.float32
            )
        )
    src_count = add(by_src)
    n_src = jnp.sum(src_count, axis=0, keepdims=True) + 1.0
    off_high, off_low = split(src_count)
    counts = [
        pick(by_src[4 * t : 4 * t + 4], lane[:NSRC]).astype(jnp.bfloat16) for t in range(tiles)
    ]
    counts = jnp.concatenate(counts + [off_high, off_low], axis=1)
    lane = lane[:per]

    def source_step(h):
        all_of(nj, over_j, a_buf.at[h], 4 + 5 * h).wait_recv()
        parts = [a_buf[h, q] for q in range(nj)]
        total = add(parts)
        src_terms = jnp.where(lane < NSRC, total / n_src, 0.0)
        both = dot(jnp.concatenate(split(src_terms[:, :NSRC]), axis=0), counts)
        along = tiles_of(both[:per] + both[per:], tiles + 2)
        for t in range(tiles):
            left = pick(parts[4 * t : 4 * t + 4], lane) - along[t]
            flat_buf[h, :, t * ROWS : (t + 1) * ROWS] = left
        flat_buf[h, :, tiles * ROWS :] = total - along[tiles] - along[tiles + 1]
        for q in range(ny):
            p_buf[h, q] = flat_buf[h, q * few : (q + 1) * few, :]
        send(ny, over_y, y, lambda p: p_buf.at[h, p], b1_buf.at[h], 5 + 5 * h)
        b1_buf[h, y] = p_buf[h, y]
        return src_terms

    def reduce_step(h):
        all_of(ny, over_y, b1_buf.at[h], 5 + 5 * h).wait_recv()
        b2_buf[h, z] = add([b1_buf[h, q] for q in range(ny)])
        send(nz, over_z, z, lambda p: b2_buf.at[h, z], b2_buf.at[h], 6 + 5 * h)

    def term_step(h):
        all_of(nz, over_z, b2_buf.at[h], 6 + 5 * h).wait_recv()
        reduced = add([b2_buf[h, q] for q in range(nz)])
        rcv_terms = reduced[:, : tiles * ROWS] / n_rcv
        high, low = split(rcv_terms)
        both = dot(high, by_rcv) + dot(low, by_rcv)
        later = reduced[:, tiles * ROWS :] - both[:, :ROWS] - both[:, ROWS:]
        c_buf[h, y] = jnp.concatenate([rcv_terms, later / n_off], axis=1)
        send(ny, over_y, y, lambda p: c_buf.at[h, y], c_buf.at[h], 7 + 5 * h)

    def back_step(h, src_terms):
        all_of(ny, over_y, c_buf.at[h], 7 + 5 * h).wait_recv()
        for q in range(ny):
            flat_buf[h, q * few : (q + 1) * few, :] = c_buf[h, q]
        off_tile = flat_buf[h, :, tiles * ROWS :]
        for t in range(tiles):
            tile = flat_buf[h, :, t * ROWS : (t + 1) * ROWS]
            for q in range(4):
                turned = tile if q == 1 else pltpu.roll(tile, (32 - 32 * q) % ROWS, 1)
                d_out[h, 4 * t + q] = jnp.where(
                    lane < NSRC, src_terms, jnp.where(lane < NSRC + NRCV, turned, off_tile)
                )
        send(nj, over_j, j, lambda p: d_out.at[h, p], terms_hbm.at[h], 8 + 5 * h)
        own = pltpu.make_async_copy(d_out.at[h, j], terms_hbm.at[h, j], load_sem.at[1 + h])
        own.start()
        stores.append(own)

    src_low = source_step(0)
    all_of(nz, over_z, gz_buf, 2).wait_recv()
    gr_buf[j] = jnp.sum(gz_buf[...], axis=0)
    send(nj, over_j, j, lambda p: gr_buf.at[j], gr_buf, 3)
    src_high = source_step(1)
    reduce_step(0)

    all_of(nj, over_j, gr_buf, 3).wait_recv()
    by_rcv = gr_buf[...]
    columns = [jnp.sum(by_rcv[q], axis=0, keepdims=True) for q in range(nj)]
    n_off = add(columns) + 1.0
    columns = [jnp.broadcast_to(c, (8, ROWS)) for c in columns]
    n_rcv = [pick(columns[4 * t : 4 * t + 4], lane[:8])[:1] for t in range(tiles)]
    n_rcv = jnp.concatenate(n_rcv, axis=1) + 1.0
    by_rcv = jnp.concatenate(split(by_rcv.reshape(nj * NRCV, ROWS)), axis=1)

    term_step(0)
    reduce_step(1)
    back_step(0, src_low)
    term_step(1)
    back_step(1, src_high)

    for phase, (n, over, buf) in enumerate(
        [(nj, over_j, ids_buf), (ny, over_y, gy_buf), (nz, over_z, gz_buf), (nj, over_j, gr_buf)]
    ):
        all_of(n, over, buf, phase).wait_send()
    for h in range(HALVES):
        for phase, (n, over, buf) in enumerate(
            [
                (nj, over_j, a_buf), (ny, over_y, b1_buf), (nz, over_z, b2_buf),
                (ny, over_y, c_buf), (nj, over_j, d_out),
            ]
        ):
            all_of(n, over, buf.at[h], 4 + 5 * h + phase).wait_send()
    for store in stores:
        store.wait()
    for h in range(HALVES):
        all_of(nj, over_j, terms_hbm.at[h], 8 + 5 * h).wait_recv()


def sweep(traces, src, rcv, off, receiver_init, offset_init, nj, ny, nz):
    traces_n, samples = traces.shape
    bins = receiver_init.shape[1]
    groups = max(1, bins // (256 * HALVES))
    chunks = HALVES * groups
    width = bins // chunks
    per = bins // nj // HALVES
    few = per // ny
    wide = nj * NRCV + ROWS
    f32, b16 = jnp.float32, jnp.bfloat16
    tables = jnp.asarray(dft_tables(samples, bins, chunks))
    anywhere = pl.BlockSpec(memory_space=pl.ANY)
    dma = pltpu.SemaphoreType.DMA
    phases = 4 + 5 * HALVES
    return pl.pallas_call(
        functools.partial(sweep_kernel, nj, ny, nz, groups),
        in_specs=[anywhere] * 7,
        out_specs=[anywhere] * 3,
        out_shape=[
            jax.ShapeDtypeStruct((chunks, traces_n, width), f32),
            jax.ShapeDtypeStruct((HALVES, nj, per, ROWS), f32),
            jax.ShapeDtypeStruct((traces_n, ROWS), b16),
        ],
        scratch_shapes=[
            pltpu.VMEM((traces_n, samples), b16),
            pltpu.VMEM((chunks, samples, 2 * width), b16),
            pltpu.VMEM((nj, 3, 1, traces_n), jnp.int32),
            pltpu.VMEM((NRCV + NOFF, bins), f32),
            pltpu.VMEM((chunks, traces_n, width), f32),
            pltpu.VMEM((traces_n, ROWS), b16),
            pltpu.VMEM((HALVES, nj, per, ROWS), f32),
            pltpu.VMEM((ny, NRCV, ROWS), f32),
            pltpu.VMEM((nz, NRCV, ROWS), f32),
            pltpu.VMEM((nj, NRCV, ROWS), f32),
            pltpu.VMEM((HALVES, nj, per, ROWS), f32),
            pltpu.VMEM((HALVES, per, wide), f32),
            pltpu.VMEM((HALVES, ny, few, wide), f32),
            pltpu.VMEM((HALVES, ny, few, wide), f32),
            pltpu.VMEM((HALVES, nz, few, wide), f32),
            pltpu.VMEM((HALVES, ny, few, wide), f32),
            pltpu.VMEM((HALVES, nj, per, ROWS), f32),
            dma((6,)), dma((chunks,)), dma((chunks,)), dma((phases,)), dma((phases,)),
        ],
        compiler_params=pltpu.CompilerParams(
            collective_id=0, has_side_effects=True, vmem_limit_bytes=60 * 1024 * 1024
        ),
    )(traces, tables, src, rcv, off, receiver_init, offset_init)


def finish_kernel(
    hot_hbm, spectra_hbm, turned_hbm, src_out, rcv_out, off_out, residual_out,
    hot_buf, x_buf, turned_buf, terms_buf, load_sem, x_sem, turned_sem, store_sem, out_sem,
):
    chunks, _, width = x_buf.shape
    load = pltpu.make_async_copy(hot_hbm, hot_buf, load_sem.at[0])
    load.start()
    parts = []
    for c in range(chunks):
        rows = pl.ds(c * width, width)
        parts.append((
            pltpu.make_async_copy(turned_hbm.at[rows], turned_buf.at[rows], turned_sem.at[c]),
            pltpu.make_async_copy(spectra_hbm.at[c], x_buf.at[c], x_sem.at[c]),
        ))
        for copy in parts[c]:
            copy.start()
    load.wait()
    hot = hot_buf[...]
    stores = []
    for c in range(chunks):
        for copy in parts[c]:
            copy.wait()
        span = slice(c * width, (c + 1) * width)
        turned = turned_buf[span]
        high, low = split(turned)
        spread = lax.dot_general(hot, high, OVER_LANES, preferred_element_type=jnp.float32)
        spread += lax.dot_general(hot, low, OVER_LANES, preferred_element_type=jnp.float32)
        x_buf[c] = x_buf[c] - spread
        store = pltpu.make_async_copy(
            x_buf.at[c], residual_out.at[0, 0, :, pl.ds(c * width, width)], store_sem.at[c]
        )
        store.start()
        stores.append(store)
        terms_buf[:, span] = turned.T
    start = 0
    for k, (out, count) in enumerate(((src_out, NSRC), (rcv_out, NRCV), (off_out, NOFF))):
        store = pltpu.make_async_copy(terms_buf.at[pl.ds(start, count)], out, out_sem.at[k])
        store.start()
        stores.append(store)
        start += count
    for store in stores:
        store.wait()


def finish(hot, spectra, turned):
    chunks, traces_n, width = spectra.shape
    bins = chunks * width
    f32 = jnp.float32
    anywhere = pl.BlockSpec(memory_space=pl.ANY)
    dma = pltpu.SemaphoreType.DMA
    return pl.pallas_call(
        finish_kernel,
        in_specs=[anywhere] * 3,
        out_specs=[anywhere] * 4,
        out_shape=[
            jax.ShapeDtypeStruct((NSRC, bins), f32),
            jax.ShapeDtypeStruct((NRCV, bins), f32),
            jax.ShapeDtypeStruct((NOFF, bins), f32),
            jax.ShapeDtypeStruct((1, 1, traces_n, bins), f32),
        ],
        scratch_shapes=[
            pltpu.VMEM(hot.shape, hot.dtype),
            pltpu.VMEM(spectra.shape, f32),
            pltpu.VMEM(turned.shape, f32),
            pltpu.VMEM((ROWS, bins), f32),
            dma((1,)), dma((chunks,)), dma((chunks,)), dma((chunks,)), dma((3,)),
        ],
        compiler_params=pltpu.CompilerParams(vmem_limit_bytes=60 * 1024 * 1024),
    )(hot, spectra, turned)


def on_device(
    nj, ny, nz, traces, source_ids, receiver_ids, offset_ids, receiver_init, offset_init
):
    src, rcv, off = source_ids[0], receiver_ids[0], offset_ids[0]
    spectra, turned, hot = sweep(
        traces[0, 0], src, rcv, off, receiver_init, offset_init, nj, ny, nz
    )
    return finish(hot, spectra, turned.reshape(-1, ROWS))


def solution(mesh):
    nsrc, nj = mesh.shape["src"], mesh.shape["rcv"]
    nz = 4 if nsrc >= 32 else 2
    ny = nsrc // nz
    placed = (
        P("src", "rcv", None, None),
        P("src", "rcv", None),
        P("src", "rcv", None),
        P("src", "rcv", None),
        P("rcv", None),
        P(),
    )
    return jax.shard_map(
        functools.partial(on_device, nj, ny, nz),
        mesh=mesh,
        in_specs=placed,
        out_specs=(P("src", None), P("rcv", None), P(), P("src", "rcv", None, None)),
        check_vma=False,
    )
```

```python
import functools

import jax
import jax.numpy as jnp
import ml_dtypes
import numpy as np
from jax import lax
from jax.experimental import pallas as pl
from jax.experimental.pallas import tpu as pltpu
from jax.sharding import PartitionSpec as P

NSRC = 32
NRCV = 32
NOFF = 64
ROWS = NSRC + NRCV + NOFF
MESH = pl.DeviceIdType.MESH
OVER_LANES = (((1,), (1,)), ((), ()))


def dft_tables(samples, bins, chunks):
    times = np.arange(samples, dtype=np.int64)[:, None]
    freqs = np.arange(bins, dtype=np.int64)[None, :]
    phase = (times * freqs) % samples
    angle = phase.astype(np.float32) * np.float32(2.0 * 3.141592653589793 / samples)
    cosine = np.cos(angle).astype(ml_dtypes.bfloat16)
    sine = (-np.sin(angle)).astype(ml_dtypes.bfloat16)
    width = bins // chunks
    return np.stack(
        [
            np.concatenate([t[:, c * width : (c + 1) * width] for t in (cosine, sine)], axis=1)
            for c in range(chunks)
        ]
    )


def hot_rows(src, rcv, off):
    parts = []
    for ids, count in ((src, NSRC), (rcv, NRCV), (off, NOFF)):
        rows = lax.broadcasted_iota(jnp.int32, (count, ids.shape[1]), 0)
        parts.append((rows == ids).astype(jnp.float32))
    return jnp.concatenate(parts, axis=0)


def split(values):
    high = values.astype(jnp.bfloat16)
    low = (values - high.astype(jnp.float32)).astype(jnp.bfloat16)
    return high, low


def dot(a, b):
    return jnp.dot(a, b, preferred_element_type=jnp.float32)


def tiles_of(values, count):
    return [values[:, t * ROWS : (t + 1) * ROWS] for t in range(count)]


def pick(tiles, lane):
    out = pltpu.roll(tiles[0], ROWS - 32, 1)
    out = jnp.where(lane < 32, out, tiles[1])
    out = jnp.where(lane < 64, out, pltpu.roll(tiles[2], 32, 1))
    return jnp.where(lane < 96, out, pltpu.roll(tiles[3], 64, 1))


HALVES = 2


def add(values):
    return functools.reduce(lambda a, b: a + b, values)


def sweep_kernel(
    nj, ny, nz, groups,
    traces_hbm, tables_hbm, src_hbm, rcv_hbm, off_hbm, rinit_hbm, oinit_hbm,
    spectra_hbm, terms_hbm, hot_hbm,
    traces_buf, tables_buf, ids_buf, init_buf, x_buf, hot_buf, sums_buf,
    gy_buf, gz_buf, gr_buf, a_buf, flat_buf, p_buf, b1_buf, b2_buf, c_buf, d_out,
    load_sem, table_sem, store_sem, send_sem, recv_sem,
):
    i = lax.axis_index("src")
    j = lax.axis_index("rcv")
    y = i // nz
    z = lax.rem(i, nz)
    samples = traces_buf.shape[1]
    width = x_buf.shape[2]
    per = a_buf.shape[2]
    few = per // ny
    tiles = nj * NRCV // ROWS
    each = nj // groups
    first = j // each

    mine = ids_buf.at[j]
    loads = [
        pltpu.make_async_copy(src_hbm, mine.at[0], load_sem.at[0]),
        pltpu.make_async_copy(rcv_hbm, mine.at[1], load_sem.at[1]),
        pltpu.make_async_copy(off_hbm, mine.at[2], load_sem.at[2]),
        pltpu.make_async_copy(traces_hbm, traces_buf, load_sem.at[3]),
        pltpu.make_async_copy(rinit_hbm, init_buf.at[pl.ds(0, NRCV)], load_sem.at[4]),
        pltpu.make_async_copy(oinit_hbm, init_buf.at[pl.ds(NRCV, NOFF)], load_sem.at[5]),
    ]
    order = [h * groups + lax.rem(first + k, groups) for h in range(HALVES) for k in range(groups)]
    tables = [
        pltpu.make_async_copy(tables_hbm.at[c], tables_buf.at[c], table_sem.at[k])
        for k, c in enumerate(order)
    ]
    for copy in loads[:4] + tables[:1] + loads[4:] + tables[1:]:
        copy.start()

    def over_j(d):
        peer = lax.rem(j + d, nj)
        return peer, (i, peer)

    def over_y(d):
        peer = lax.rem(y + d, ny)
        return peer, (peer * nz + z, j)

    def over_z(d):
        peer = lax.rem(z + d, nz)
        return peer, (y * nz + peer, j)

    def copy_to(device, source, target, phase):
        return pltpu.make_async_remote_copy(
            src_ref=source, dst_ref=target, send_sem=send_sem.at[phase],
            recv_sem=recv_sem.at[phase], device_id=device, device_id_type=MESH,
        )

    def send(n, over, me, source, buf, phase):
        for d in range(1, n):
            peer, device = over(d)
            copy_to(device, source(peer), buf.at[me], phase).start()

    def all_of(n, over, buf, phase):
        part = buf.at[pl.ds(0, n - 1)]
        return copy_to(over(1)[1], part, part, phase)

    barrier = pltpu.get_barrier_semaphore()
    for n, over in ((ny, over_y), (nj, over_j), (nz, over_z)):
        for d in range(1, n):
            pl.semaphore_signal(barrier, inc=1, device_id=over(d)[1], device_id_type=MESH)

    for copy in loads[:3]:
        copy.wait()
    hot = hot_rows(ids_buf[j, 0], ids_buf[j, 1], ids_buf[j, 2])
    hot_buf[...] = hot.T.astype(jnp.bfloat16)
    hot = hot.astype(jnp.bfloat16)
    gram = lax.dot_general(hot, hot, OVER_LANES, preferred_element_type=jnp.float32)
    gy_buf[y] = gram[NSRC : NSRC + NRCV]
    row = lax.broadcasted_iota(jnp.int32, (ROWS, ROWS), 0)
    lane = lax.broadcasted_iota(jnp.int32, (ROWS, ROWS), 1)
    from_rcv = (lane >= NSRC) & (lane < NSRC + NRCV) & (row < NSRC)
    from_off = (lane >= NSRC + NRCV) & (row < NSRC + NRCV)
    before = jnp.where(from_rcv | from_off, gram, 0.0).astype(jnp.bfloat16)[:, NSRC:]
    pl.semaphore_wait(barrier, nj + ny + nz - 3)
    send(nj, over_j, j, lambda p: ids_buf.at[j], ids_buf, 0)
    stores = [pltpu.make_async_copy(hot_buf, hot_hbm, load_sem.at[0])]
    stores[0].start()

    for copy in loads[3:]:
        copy.wait()
    for n, c in enumerate(order):
        h, k = n // groups, n % groups
        g = c - h * groups
        tables[n].wait()
        both = dot(traces_buf[...], tables_buf[c])
        real, imag = both[:, :width], both[:, width:]
        spectra = 0.5 * jnp.log((real * real + imag * imag) * (1.0 / samples) + 0.25)
        x_buf[c] = spectra
        store = pltpu.make_async_copy(x_buf.at[c], spectra_hbm.at[c], store_sem.at[n])
        store.start()
        stores.append(store)
        init = init_buf[:, pl.ds(pl.multiple_of(c * width, width), width)]
        spec_high, spec_low = split(spectra)
        init_high, init_low = split(init)
        sums = (dot(hot, spec_high) - dot(before, init_high)) + (
            dot(hot, spec_low) - dot(before, init_low)
        )
        turned = sums.T
        for q in range(each):
            sums_buf[h, g * each + q] = turned[q * per : (q + 1) * per]
        for q in range(1 if k == 0 else 0, each):
            peer = g * each + (lax.rem(j + q, each) if k == 0 else q)
            copy_to((i, peer), sums_buf.at[h, peer], a_buf.at[h, j], 4 + 5 * h).start()
        if n == groups - 1:
            send(ny, over_y, y, lambda p: gy_buf.at[y], gy_buf, 1)
    for h in range(HALVES):
        a_buf[h, j] = sums_buf[h, j]

    all_of(nj, over_j, ids_buf, 0).wait_recv()
    by_src = []
    for q in range(nj):
        peer_hot = hot_rows(ids_buf[q, 0], ids_buf[q, 1], ids_buf[q, 2]).astype(jnp.bfloat16)
        by_src.append(
            lax.dot_general(
                peer_hot[:NSRC], peer_hot, OVER_LANES, preferred_element_type=jnp.float32
            )
        )
    src_count = add(by_src)
    n_src = jnp.sum(src_count, axis=0, keepdims=True) + 1.0
    off_high, off_low = split(src_count)
    counts = [
        pick(by_src[4 * t : 4 * t + 4], lane[:NSRC]).astype(jnp.bfloat16) for t in range(tiles)
    ]
    counts = jnp.concatenate(counts + [off_high, off_low], axis=1)
    lane = lane[:per]
    all_of(ny, over_y, gy_buf, 1).wait_recv()
    gz_buf[z] = jnp.sum(gy_buf[...], axis=0)
    send(nz, over_z, z, lambda p: gz_buf.at[z], gz_buf, 2)

    def source_step(h):
        all_of(nj, over_j, a_buf.at[h], 4 + 5 * h).wait_recv()
        parts = [a_buf[h, q] for q in range(nj)]
        total = add(parts)
        src_terms = jnp.where(lane < NSRC, total / n_src, 0.0)
        both = dot(jnp.concatenate(split(src_terms[:, :NSRC]), axis=0), counts)
        along = tiles_of(both[:per] + both[per:], tiles + 2)
        for t in range(tiles):
            left = pick(parts[4 * t : 4 * t + 4], lane) - along[t]
            flat_buf[h, :, t * ROWS : (t + 1) * ROWS] = left
        flat_buf[h, :, tiles * ROWS :] = total - along[tiles] - along[tiles + 1]
        for q in range(ny):
            p_buf[h, q] = flat_buf[h, q * few : (q + 1) * few, :]
        send(ny, over_y, y, lambda p: p_buf.at[h, p], b1_buf.at[h], 5 + 5 * h)
        b1_buf[h, y] = p_buf[h, y]
        return src_terms

    def reduce_step(h):
        all_of(ny, over_y, b1_buf.at[h], 5 + 5 * h).wait_recv()
        b2_buf[h, z] = add([b1_buf[h, q] for q in range(ny)])
        send(nz, over_z, z, lambda p: b2_buf.at[h, z], b2_buf.at[h], 6 + 5 * h)

    def term_step(h):
        all_of(nz, over_z, b2_buf.at[h], 6 + 5 * h).wait_recv()
        reduced = add([b2_buf[h, q] for q in range(nz)])
        rcv_terms = reduced[:, : tiles * ROWS] / n_rcv
        high, low = split(rcv_terms)
        both = dot(high, by_rcv) + dot(low, by_rcv)
        later = reduced[:, tiles * ROWS :] - both[:, :ROWS] - both[:, ROWS:]
        c_buf[h, y] = jnp.concatenate([rcv_terms, later / n_off], axis=1)
        send(ny, over_y, y, lambda p: c_buf.at[h, y], c_buf.at[h], 7 + 5 * h)

    def back_step(h, src_terms):
        all_of(ny, over_y, c_buf.at[h], 7 + 5 * h).wait_recv()
        for q in range(ny):
            flat_buf[h, q * few : (q + 1) * few, :] = c_buf[h, q]
        off_tile = flat_buf[h, :, tiles * ROWS :]
        for t in range(tiles):
            tile = flat_buf[h, :, t * ROWS : (t + 1) * ROWS]
            for q in range(4):
                turned = tile if q == 1 else pltpu.roll(tile, (32 - 32 * q) % ROWS, 1)
                d_out[h, 4 * t + q] = jnp.where(
                    lane < NSRC, src_terms, jnp.where(lane < NSRC + NRCV, turned, off_tile)
                )
        send(nj, over_j, j, lambda p: d_out.at[h, p], terms_hbm.at[h], 8 + 5 * h)
        own = pltpu.make_async_copy(d_out.at[h, j], terms_hbm.at[h, j], load_sem.at[1 + h])
        own.start()
        stores.append(own)

    src_low = source_step(0)
    src_high = source_step(1)
    all_of(nz, over_z, gz_buf, 2).wait_recv()
    gr_buf[j] = jnp.sum(gz_buf[...], axis=0)
    send(nj, over_j, j, lambda p: gr_buf.at[j], gr_buf, 3)
    reduce_step(0)
    reduce_step(1)

    all_of(nj, over_j, gr_buf, 3).wait_recv()
    by_rcv = gr_buf[...]
    columns = [jnp.sum(by_rcv[q], axis=0, keepdims=True) for q in range(nj)]
    n_off = add(columns) + 1.0
    columns = [jnp.broadcast_to(c, (8, ROWS)) for c in columns]
    n_rcv = [pick(columns[4 * t : 4 * t + 4], lane[:8])[:1] for t in range(tiles)]
    n_rcv = jnp.concatenate(n_rcv, axis=1) + 1.0
    by_rcv = jnp.concatenate(split(by_rcv.reshape(nj * NRCV, ROWS)), axis=1)

    term_step(0)
    term_step(1)
    back_step(0, src_low)
    back_step(1, src_high)

    for phase, (n, over, buf) in enumerate(
        [(nj, over_j, ids_buf), (ny, over_y, gy_buf), (nz, over_z, gz_buf), (nj, over_j, gr_buf)]
    ):
        all_of(n, over, buf, phase).wait_send()
    for h in range(HALVES):
        for phase, (n, over, buf) in enumerate(
            [
                (nj, over_j, a_buf), (ny, over_y, b1_buf), (nz, over_z, b2_buf),
                (ny, over_y, c_buf), (nj, over_j, d_out),
            ]
        ):
            all_of(n, over, buf.at[h], 4 + 5 * h + phase).wait_send()
    for store in stores:
        store.wait()
    for h in range(HALVES):
        all_of(nj, over_j, terms_hbm.at[h], 8 + 5 * h).wait_recv()


def sweep(traces, src, rcv, off, receiver_init, offset_init, nj, ny, nz):
    traces_n, samples = traces.shape
    bins = receiver_init.shape[1]
    groups = max(1, bins // (256 * HALVES))
    chunks = HALVES * groups
    width = bins // chunks
    per = bins // nj // HALVES
    few = per // ny
    wide = nj * NRCV + ROWS
    f32, b16 = jnp.float32, jnp.bfloat16
    tables = jnp.asarray(dft_tables(samples, bins, chunks))
    anywhere = pl.BlockSpec(memory_space=pl.ANY)
    dma = pltpu.SemaphoreType.DMA
    phases = 4 + 5 * HALVES
    return pl.pallas_call(
        functools.partial(sweep_kernel, nj, ny, nz, groups),
        in_specs=[anywhere] * 7,
        out_specs=[anywhere] * 3,
        out_shape=[
            jax.ShapeDtypeStruct((chunks, traces_n, width), f32),
            jax.ShapeDtypeStruct((HALVES, nj, per, ROWS), f32),
            jax.ShapeDtypeStruct((traces_n, ROWS), b16),
        ],
        scratch_shapes=[
            pltpu.VMEM((traces_n, samples), b16),
            pltpu.VMEM((chunks, samples, 2 * width), b16),
            pltpu.VMEM((nj, 3, 1, traces_n), jnp.int32),
            pltpu.VMEM((NRCV + NOFF, bins), f32),
            pltpu.VMEM((chunks, traces_n, width), f32),
            pltpu.VMEM((traces_n, ROWS), b16),
            pltpu.VMEM((HALVES, nj, per, ROWS), f32),
            pltpu.VMEM((ny, NRCV, ROWS), f32),
            pltpu.VMEM((nz, NRCV, ROWS), f32),
            pltpu.VMEM((nj, NRCV, ROWS), f32),
            pltpu.VMEM((HALVES, nj, per, ROWS), f32),
            pltpu.VMEM((HALVES, per, wide), f32),
            pltpu.VMEM((HALVES, ny, few, wide), f32),
            pltpu.VMEM((HALVES, ny, few, wide), f32),
            pltpu.VMEM((HALVES, nz, few, wide), f32),
            pltpu.VMEM((HALVES, ny, few, wide), f32),
            pltpu.VMEM((HALVES, nj, per, ROWS), f32),
            dma((6,)), dma((chunks,)), dma((chunks,)), dma((phases,)), dma((phases,)),
        ],
        compiler_params=pltpu.CompilerParams(
            collective_id=0, has_side_effects=True, vmem_limit_bytes=60 * 1024 * 1024
        ),
    )(traces, tables, src, rcv, off, receiver_init, offset_init)


def finish_kernel(
    hot_hbm, spectra_hbm, turned_hbm, src_out, rcv_out, off_out, residual_out,
    hot_buf, x_buf, turned_buf, terms_buf, load_sem, x_sem, turned_sem, store_sem, out_sem,
):
    chunks, _, width = x_buf.shape
    load = pltpu.make_async_copy(hot_hbm, hot_buf, load_sem.at[0])
    load.start()
    parts = []
    for c in range(chunks):
        rows = pl.ds(c * width, width)
        parts.append((
            pltpu.make_async_copy(turned_hbm.at[rows], turned_buf.at[rows], turned_sem.at[c]),
            pltpu.make_async_copy(spectra_hbm.at[c], x_buf.at[c], x_sem.at[c]),
        ))
        for copy in parts[c]:
            copy.start()
    load.wait()
    hot = hot_buf[...]
    stores = []
    for c in range(chunks):
        for copy in parts[c]:
            copy.wait()
        span = slice(c * width, (c + 1) * width)
        turned = turned_buf[span]
        high, low = split(turned)
        spread = lax.dot_general(hot, high, OVER_LANES, preferred_element_type=jnp.float32)
        spread += lax.dot_general(hot, low, OVER_LANES, preferred_element_type=jnp.float32)
        x_buf[c] = x_buf[c] - spread
        store = pltpu.make_async_copy(
            x_buf.at[c], residual_out.at[0, 0, :, pl.ds(c * width, width)], store_sem.at[c]
        )
        store.start()
        stores.append(store)
        terms_buf[:, span] = turned.T
    start = 0
    for k, (out, count) in enumerate(((src_out, NSRC), (rcv_out, NRCV), (off_out, NOFF))):
        store = pltpu.make_async_copy(terms_buf.at[pl.ds(start, count)], out, out_sem.at[k])
        store.start()
        stores.append(store)
        start += count
    for store in stores:
        store.wait()


def finish(hot, spectra, turned):
    chunks, traces_n, width = spectra.shape
    bins = chunks * width
    f32 = jnp.float32
    anywhere = pl.BlockSpec(memory_space=pl.ANY)
    dma = pltpu.SemaphoreType.DMA
    return pl.pallas_call(
        finish_kernel,
        in_specs=[anywhere] * 3,
        out_specs=[anywhere] * 4,
        out_shape=[
            jax.ShapeDtypeStruct((NSRC, bins), f32),
            jax.ShapeDtypeStruct((NRCV, bins), f32),
            jax.ShapeDtypeStruct((NOFF, bins), f32),
            jax.ShapeDtypeStruct((1, 1, traces_n, bins), f32),
        ],
        scratch_shapes=[
            pltpu.VMEM(hot.shape, hot.dtype),
            pltpu.VMEM(spectra.shape, f32),
            pltpu.VMEM(turned.shape, f32),
            pltpu.VMEM((ROWS, bins), f32),
            dma((1,)), dma((chunks,)), dma((chunks,)), dma((chunks,)), dma((3,)),
        ],
        compiler_params=pltpu.CompilerParams(vmem_limit_bytes=60 * 1024 * 1024),
    )(hot, spectra, turned)


def on_device(
    nj, ny, nz, traces, source_ids, receiver_ids, offset_ids, receiver_init, offset_init
):
    src, rcv, off = source_ids[0], receiver_ids[0], offset_ids[0]
    spectra, turned, hot = sweep(
        traces[0, 0], src, rcv, off, receiver_init, offset_init, nj, ny, nz
    )
    return finish(hot, spectra, turned.reshape(-1, ROWS))


def solution(mesh):
    nsrc, nj = mesh.shape["src"], mesh.shape["rcv"]
    nz = 4 if nsrc >= 32 else 2
    ny = nsrc // nz
    placed = (
        P("src", "rcv", None, None),
        P("src", "rcv", None),
        P("src", "rcv", None),
        P("src", "rcv", None),
        P("rcv", None),
        P(),
    )
    return jax.shard_map(
        functools.partial(on_device, nj, ny, nz),
        mesh=mesh,
        in_specs=placed,
        out_specs=(P("src", None), P("rcv", None), P(), P("src", "rcv", None, None)),
        check_vma=False,
    )
```

```python
import functools

import jax
import jax.numpy as jnp
import ml_dtypes
import numpy as np
from jax import lax
from jax.experimental import pallas as pl
from jax.experimental.pallas import tpu as pltpu
from jax.sharding import PartitionSpec as P

NSRC = 32
NRCV = 32
NOFF = 64
ROWS = NSRC + NRCV + NOFF
MESH = pl.DeviceIdType.MESH
OVER_LANES = (((1,), (1,)), ((), ()))


def dft_tables(samples, bins, chunks):
    times = np.arange(samples, dtype=np.int64)[:, None]
    freqs = np.arange(bins, dtype=np.int64)[None, :]
    phase = (times * freqs) % samples
    angle = phase.astype(np.float32) * np.float32(2.0 * 3.141592653589793 / samples)
    cosine = np.cos(angle).astype(ml_dtypes.bfloat16)
    sine = (-np.sin(angle)).astype(ml_dtypes.bfloat16)
    width = bins // chunks
    return np.stack(
        [
            np.concatenate([t[:, c * width : (c + 1) * width] for t in (cosine, sine)], axis=1)
            for c in range(chunks)
        ]
    )


def hot_rows(src, rcv, off):
    parts = []
    for ids, count in ((src, NSRC), (rcv, NRCV), (off, NOFF)):
        rows = lax.broadcasted_iota(jnp.int32, (count, ids.shape[1]), 0)
        parts.append((rows == ids).astype(jnp.float32))
    return jnp.concatenate(parts, axis=0)


def split(values):
    high = values.astype(jnp.bfloat16)
    low = (values - high.astype(jnp.float32)).astype(jnp.bfloat16)
    return high, low


def dot(a, b):
    return jnp.dot(a, b, preferred_element_type=jnp.float32)


def tiles_of(values, count):
    return [values[:, t * ROWS : (t + 1) * ROWS] for t in range(count)]


def pick(tiles, lane):
    out = pltpu.roll(tiles[0], ROWS - 32, 1)
    out = jnp.where(lane < 32, out, tiles[1])
    out = jnp.where(lane < 64, out, pltpu.roll(tiles[2], 32, 1))
    return jnp.where(lane < 96, out, pltpu.roll(tiles[3], 64, 1))


HALVES = 2


def add(values):
    return functools.reduce(lambda a, b: a + b, values)


def sweep_kernel(
    nj, ny, nz, groups,
    traces_hbm, tables_hbm, src_hbm, rcv_hbm, off_hbm, rinit_hbm, oinit_hbm,
    spectra_hbm, terms_hbm, hot_hbm,
    traces_buf, tables_buf, ids_buf, init_buf, x_buf, hot_buf, sums_buf,
    gy_buf, gz_buf, gr_buf, a_buf, s_buf, flat_buf, p_buf, b1_buf, b2_buf, c_buf, d_out,
    load_sem, table_sem, store_sem, send_sem, recv_sem,
):
    i = lax.axis_index("src")
    j = lax.axis_index("rcv")
    y = i // nz
    z = lax.rem(i, nz)
    samples = traces_buf.shape[1]
    width = x_buf.shape[2]
    per = a_buf.shape[2]
    few = per // ny
    quarter = per // 4
    tiles = nj * NRCV // ROWS
    each = nj // groups
    first = j // each

    mine = ids_buf.at[j]
    loads = [
        pltpu.make_async_copy(src_hbm, mine.at[0], load_sem.at[0]),
        pltpu.make_async_copy(rcv_hbm, mine.at[1], load_sem.at[1]),
        pltpu.make_async_copy(off_hbm, mine.at[2], load_sem.at[2]),
        pltpu.make_async_copy(traces_hbm, traces_buf, load_sem.at[3]),
        pltpu.make_async_copy(rinit_hbm, init_buf.at[pl.ds(0, NRCV)], load_sem.at[4]),
        pltpu.make_async_copy(oinit_hbm, init_buf.at[pl.ds(NRCV, NOFF)], load_sem.at[5]),
    ]
    order = [h * groups + lax.rem(first + k, groups) for h in range(HALVES) for k in range(groups)]
    tables = [
        pltpu.make_async_copy(tables_hbm.at[c], tables_buf.at[c], table_sem.at[k])
        for k, c in enumerate(order)
    ]
    for copy in loads[:4] + tables[:1] + loads[4:] + tables[1:]:
        copy.start()

    def over_j(d):
        peer = lax.rem(j + d, nj)
        return peer, (i, peer)

    def over_y(d):
        peer = lax.rem(y + d, ny)
        return peer, (peer * nz + z, j)

    def over_z(d):
        peer = lax.rem(z + d, nz)
        return peer, (y * nz + peer, j)

    def copy_to(device, source, target, phase):
        return pltpu.make_async_remote_copy(
            src_ref=source, dst_ref=target, send_sem=send_sem.at[phase],
            recv_sem=recv_sem.at[phase], device_id=device, device_id_type=MESH,
        )

    def send(n, over, me, source, buf, phase):
        for d in range(1, n):
            peer, device = over(d)
            copy_to(device, source(peer), buf.at[me], phase).start()

    def all_of(n, over, buf, phase):
        part = buf.at[pl.ds(0, n - 1)]
        return copy_to(over(1)[1], part, part, phase)

    barrier = pltpu.get_barrier_semaphore()
    for n, over in ((ny, over_y), (nj, over_j), (nz, over_z)):
        for d in range(1, n):
            pl.semaphore_signal(barrier, inc=1, device_id=over(d)[1], device_id_type=MESH)

    for copy in loads[:3]:
        copy.wait()
    hot = hot_rows(ids_buf[j, 0], ids_buf[j, 1], ids_buf[j, 2])
    hot_buf[...] = hot.T.astype(jnp.bfloat16)
    hot = hot.astype(jnp.bfloat16)
    gram = lax.dot_general(hot, hot, OVER_LANES, preferred_element_type=jnp.float32)
    gy_buf[y] = gram[NSRC : NSRC + NRCV]
    row = lax.broadcasted_iota(jnp.int32, (ROWS, ROWS), 0)
    lane = lax.broadcasted_iota(jnp.int32, (ROWS, ROWS), 1)
    from_rcv = (lane >= NSRC) & (lane < NSRC + NRCV) & (row < NSRC)
    from_off = (lane >= NSRC + NRCV) & (row < NSRC + NRCV)
    before = jnp.where(from_rcv | from_off, gram, 0.0).astype(jnp.bfloat16)[:, NSRC:]
    pl.semaphore_wait(barrier, nj + ny + nz - 3)
    send(nj, over_j, j, lambda p: ids_buf.at[j], ids_buf, 0)
    stores = [pltpu.make_async_copy(hot_buf, hot_hbm, load_sem.at[0])]
    stores[0].start()

    for copy in loads[3:]:
        copy.wait()
    for n, c in enumerate(order):
        h, k = n // groups, n % groups
        g = c - h * groups
        tables[n].wait()
        both = dot(traces_buf[...], tables_buf[c])
        real, imag = both[:, :width], both[:, width:]
        spectra = 0.5 * jnp.log((real * real + imag * imag) * (1.0 / samples) + 0.25)
        x_buf[c] = spectra
        store = pltpu.make_async_copy(x_buf.at[c], spectra_hbm.at[c], store_sem.at[n])
        store.start()
        stores.append(store)
        init = init_buf[:, pl.ds(pl.multiple_of(c * width, width), width)]
        spec_high, spec_low = split(spectra)
        init_high, init_low = split(init)
        sums = (dot(hot, spec_high) - dot(before, init_high)) + (
            dot(hot, spec_low) - dot(before, init_low)
        )
        turned = sums.T
        for q in range(each):
            sums_buf[h, g * each + q] = turned[q * per : (q + 1) * per]
        for q in range(1 if k == 0 else 0, each):
            peer = g * each + (lax.rem(j + q, each) if k == 0 else q)
            copy_to((i, peer), sums_buf.at[h, peer], a_buf.at[h, j], 4 + 5 * h).start()
        if n == groups - 1:
            send(ny, over_y, y, lambda p: gy_buf.at[y], gy_buf, 1)
    for h in range(HALVES):
        a_buf[h, j] = sums_buf[h, j]

    all_of(nj, over_j, ids_buf, 0).wait_recv()
    by_src = []
    for q in range(nj):
        peer_hot = hot_rows(ids_buf[q, 0], ids_buf[q, 1], ids_buf[q, 2]).astype(jnp.bfloat16)
        by_src.append(
            lax.dot_general(
                peer_hot[:NSRC], peer_hot, OVER_LANES, preferred_element_type=jnp.float32
            )
        )
    src_count = add(by_src)
    n_src = jnp.sum(src_count, axis=0, keepdims=True) + 1.0
    off_high, off_low = split(src_count)
    counts = [
        pick(by_src[4 * t : 4 * t + 4], lane[:NSRC]).astype(jnp.bfloat16) for t in range(tiles)
    ]
    counts = jnp.concatenate(counts + [off_high, off_low], axis=1)
    lane = lane[:per]
    all_of(ny, over_y, gy_buf, 1).wait_recv()
    gz_buf[z] = jnp.sum(gy_buf[...], axis=0)
    send(nz, over_z, z, lambda p: gz_buf.at[z], gz_buf, 2)

    def source_step(h):
        all_of(nj, over_j, a_buf.at[h], 4 + 5 * h).wait_recv()
        parts = [a_buf[h, q] for q in range(nj)]
        total = add(parts)
        src_terms = jnp.where(lane < NSRC, total / n_src, 0.0)
        both = dot(jnp.concatenate(split(src_terms[:, :NSRC]), axis=0), counts)
        along = tiles_of(both[:per] + both[per:], tiles + 2)
        for t in range(tiles):
            left = pick(parts[4 * t : 4 * t + 4], lane) - along[t]
            flat_buf[h, :, t * ROWS : (t + 1) * ROWS] = left
        flat_buf[h, :, tiles * ROWS :] = total - along[tiles] - along[tiles + 1]
        for q in range(ny):
            p_buf[h, q] = flat_buf[h, q * few : (q + 1) * few, :]
        send(ny, over_y, y, lambda p: p_buf.at[h, p], b1_buf.at[h], 5 + 5 * h)
        b1_buf[h, y] = p_buf[h, y]
        groups_of = [src_terms[q * quarter : (q + 1) * quarter] for q in range(4)]
        s_buf[h] = add([groups_of[0]] + [pltpu.roll(groups_of[q], 32 * q, 1) for q in (1, 2, 3)])

    def reduce_step(h):
        all_of(ny, over_y, b1_buf.at[h], 5 + 5 * h).wait_recv()
        b2_buf[h, z] = add([b1_buf[h, q] for q in range(ny)])
        send(nz, over_z, z, lambda p: b2_buf.at[h, z], b2_buf.at[h], 6 + 5 * h)

    def term_step(h):
        all_of(nz, over_z, b2_buf.at[h], 6 + 5 * h).wait_recv()
        reduced = add([b2_buf[h, q] for q in range(nz)])
        rcv_terms = reduced[:, : tiles * ROWS] / n_rcv
        high, low = split(rcv_terms)
        both = dot(high, by_rcv) + dot(low, by_rcv)
        later = reduced[:, tiles * ROWS :] - both[:, :ROWS] - both[:, ROWS:]
        c_buf[h, y] = jnp.concatenate([rcv_terms, later / n_off], axis=1)
        send(ny, over_y, y, lambda p: c_buf.at[h, y], c_buf.at[h], 7 + 5 * h)

    def source_out(h):
        send(
            nj, over_j, j, lambda p: s_buf.at[h],
            terms_hbm.at[h, :, pl.ds(3 * quarter, quarter)], 4 + 5 * HALVES + h,
        )
        own = pltpu.make_async_copy(
            s_buf.at[h], terms_hbm.at[h, j, pl.ds(3 * quarter, quarter)], load_sem.at[3 + h]
        )
        own.start()
        stores.append(own)

    def back_step(h):
        all_of(ny, over_y, c_buf.at[h], 7 + 5 * h).wait_recv()
        for q in range(ny):
            flat_buf[h, q * few : (q + 1) * few, :] = c_buf[h, q]
        off_tile = flat_buf[h, :, tiles * ROWS :]
        off_fill = [pltpu.roll(off_tile[3 * quarter :], shift, 1) for shift in (64, 32)]
        for t in range(tiles):
            tile = flat_buf[h, :, t * ROWS : (t + 1) * ROWS]
            for q in range(4):
                turned = tile if q == 1 else pltpu.roll(tile, (32 - 32 * q) % ROWS, 1)
                fill = [pltpu.roll(turned[3 * quarter :], 96, 1)] + off_fill
                whole = jnp.where(lane < NSRC + NRCV, turned, off_tile)
                for k in range(3):
                    rows = slice(k * quarter, (k + 1) * quarter)
                    d_out[h, 4 * t + q, rows, :] = jnp.where(
                        lane[:quarter] < 32, fill[k], whole[rows]
                    )
        back = terms_hbm.at[h, :, pl.ds(0, 3 * quarter)]
        send(nj, over_j, j, lambda p: d_out.at[h, p], back, 8 + 5 * h)
        own = pltpu.make_async_copy(d_out.at[h, j], back.at[j], load_sem.at[1 + h])
        own.start()
        stores.append(own)

    source_step(0)
    source_step(1)
    all_of(nz, over_z, gz_buf, 2).wait_recv()
    count = jnp.sum(gz_buf[...], axis=0)
    half = NRCV // 2
    wide = lax.broadcasted_iota(jnp.int32, (half, ROWS), 1) >= NSRC + NRCV
    gr_buf[j] = jnp.where(wide, count[:half], pltpu.roll(count[half:], ROWS // 2, 1))
    send(nj, over_j, j, lambda p: gr_buf.at[j], gr_buf, 3)
    for h in range(HALVES):
        source_out(h)
    reduce_step(0)
    reduce_step(1)

    all_of(nj, over_j, gr_buf, 3).wait_recv()
    by_rcv = []
    for q in range(nj):
        packed = gr_buf[q]
        by_rcv.append(jnp.where(wide, packed, 0.0))
        by_rcv.append(jnp.where(wide, pltpu.roll(packed, ROWS // 2, 1), 0.0))
    by_rcv = jnp.concatenate(by_rcv, axis=0)
    n_off = jnp.sum(by_rcv, axis=0, keepdims=True) + 1.0
    by_rcv = split(by_rcv)
    ones = jnp.ones((16, ROWS), jnp.bfloat16)
    n_rcv = add(
        [
            lax.dot_general(ones, part, OVER_LANES, preferred_element_type=jnp.float32)
            for part in by_rcv
        ]
    )[:1] + 1.0
    by_rcv = jnp.concatenate(by_rcv, axis=1)

    term_step(0)
    term_step(1)
    back_step(0)
    back_step(1)

    for phase, (n, over, buf) in enumerate(
        [(nj, over_j, ids_buf), (ny, over_y, gy_buf), (nz, over_z, gz_buf), (nj, over_j, gr_buf)]
    ):
        all_of(n, over, buf, phase).wait_send()
    for h in range(HALVES):
        for phase, (n, over, buf) in enumerate(
            [
                (nj, over_j, a_buf), (ny, over_y, b1_buf), (nz, over_z, b2_buf),
                (ny, over_y, c_buf), (nj, over_j, d_out),
            ]
        ):
            all_of(n, over, buf.at[h], 4 + 5 * h + phase).wait_send()
        sources = terms_hbm.at[h, :, pl.ds(3 * quarter, quarter)]
        all_of(nj, over_j, sources, 4 + 5 * HALVES + h).wait_send()
        all_of(nj, over_j, sources, 4 + 5 * HALVES + h).wait_recv()
    for store in stores:
        store.wait()
    for h in range(HALVES):
        all_of(nj, over_j, terms_hbm.at[h, :, pl.ds(0, 3 * quarter)], 8 + 5 * h).wait_recv()


def sweep(traces, src, rcv, off, receiver_init, offset_init, nj, ny, nz):
    traces_n, samples = traces.shape
    bins = receiver_init.shape[1]
    groups = max(1, bins // (256 * HALVES))
    chunks = HALVES * groups
    width = bins // chunks
    per = bins // nj // HALVES
    few = per // ny
    wide = nj * NRCV + ROWS
    f32, b16 = jnp.float32, jnp.bfloat16
    tables = jnp.asarray(dft_tables(samples, bins, chunks))
    anywhere = pl.BlockSpec(memory_space=pl.ANY)
    dma = pltpu.SemaphoreType.DMA
    phases = 4 + 6 * HALVES
    return pl.pallas_call(
        functools.partial(sweep_kernel, nj, ny, nz, groups),
        in_specs=[anywhere] * 7,
        out_specs=[anywhere] * 3,
        out_shape=[
            jax.ShapeDtypeStruct((chunks, traces_n, width), f32),
            jax.ShapeDtypeStruct((HALVES, nj, per, ROWS), f32),
            jax.ShapeDtypeStruct((traces_n, ROWS), b16),
        ],
        scratch_shapes=[
            pltpu.VMEM((traces_n, samples), b16),
            pltpu.VMEM((chunks, samples, 2 * width), b16),
            pltpu.VMEM((nj, 3, 1, traces_n), jnp.int32),
            pltpu.VMEM((NRCV + NOFF, bins), f32),
            pltpu.VMEM((chunks, traces_n, width), f32),
            pltpu.VMEM((traces_n, ROWS), b16),
            pltpu.VMEM((HALVES, nj, per, ROWS), f32),
            pltpu.VMEM((ny, NRCV, ROWS), f32),
            pltpu.VMEM((nz, NRCV, ROWS), f32),
            pltpu.VMEM((nj, NRCV // 2, ROWS), f32),
            pltpu.VMEM((HALVES, nj, per, ROWS), f32),
            pltpu.VMEM((HALVES, per // 4, ROWS), f32),
            pltpu.VMEM((HALVES, per, wide), f32),
            pltpu.VMEM((HALVES, ny, few, wide), f32),
            pltpu.VMEM((HALVES, ny, few, wide), f32),
            pltpu.VMEM((HALVES, nz, few, wide), f32),
            pltpu.VMEM((HALVES, ny, few, wide), f32),
            pltpu.VMEM((HALVES, nj, per // 4 * 3, ROWS), f32),
            dma((6,)), dma((chunks,)), dma((chunks,)), dma((phases,)), dma((phases,)),
        ],
        compiler_params=pltpu.CompilerParams(
            collective_id=0, has_side_effects=True, vmem_limit_bytes=60 * 1024 * 1024
        ),
    )(traces, tables, src, rcv, off, receiver_init, offset_init)


def unpack(packed, per):
    quarter = per // 4
    lane = lax.broadcasted_iota(jnp.int32, (quarter, ROWS), 1)
    out = []
    for start in range(0, packed.shape[0], per):
        rows = [packed[start + k * quarter : start + (k + 1) * quarter] for k in range(4)]
        sources = rows[3]
        out.append(jnp.where(lane < 32, sources, rows[0]))
        out.append(jnp.where(lane < 32, pltpu.roll(sources, 96, 1), rows[1]))
        out.append(jnp.where(lane < 32, pltpu.roll(sources, 64, 1), rows[2]))
        last = jnp.where(lane < 96, pltpu.roll(rows[1], 64, 1), pltpu.roll(rows[2], 96, 1))
        last = jnp.where(lane < 64, pltpu.roll(rows[0], 32, 1), last)
        out.append(jnp.where(lane < 32, pltpu.roll(sources, 32, 1), last))
    return jnp.concatenate(out, axis=0)


def finish_kernel(
    per, hot_hbm, spectra_hbm, turned_hbm, src_out, rcv_out, off_out, residual_out,
    hot_buf, x_buf, turned_buf, terms_buf, load_sem, x_sem, turned_sem, store_sem, out_sem,
):
    chunks, _, width = x_buf.shape
    load = pltpu.make_async_copy(hot_hbm, hot_buf, load_sem.at[0])
    load.start()
    parts = []
    for c in range(chunks):
        rows = pl.ds(c * width, width)
        parts.append((
            pltpu.make_async_copy(turned_hbm.at[rows], turned_buf.at[rows], turned_sem.at[c]),
            pltpu.make_async_copy(spectra_hbm.at[c], x_buf.at[c], x_sem.at[c]),
        ))
        for copy in parts[c]:
            copy.start()
    load.wait()
    hot = hot_buf[...]
    stores = []
    for c in range(chunks):
        for copy in parts[c]:
            copy.wait()
        span = slice(c * width, (c + 1) * width)
        turned = unpack(turned_buf[span], per)
        high, low = split(turned)
        spread = lax.dot_general(hot, high, OVER_LANES, preferred_element_type=jnp.float32)
        spread += lax.dot_general(hot, low, OVER_LANES, preferred_element_type=jnp.float32)
        x_buf[c] = x_buf[c] - spread
        store = pltpu.make_async_copy(
            x_buf.at[c], residual_out.at[0, 0, :, pl.ds(c * width, width)], store_sem.at[c]
        )
        store.start()
        stores.append(store)
        terms_buf[:, span] = turned.T
    start = 0
    for k, (out, count) in enumerate(((src_out, NSRC), (rcv_out, NRCV), (off_out, NOFF))):
        store = pltpu.make_async_copy(terms_buf.at[pl.ds(start, count)], out, out_sem.at[k])
        store.start()
        stores.append(store)
        start += count
    for store in stores:
        store.wait()


def finish(hot, spectra, turned, per):
    chunks, traces_n, width = spectra.shape
    bins = chunks * width
    f32 = jnp.float32
    anywhere = pl.BlockSpec(memory_space=pl.ANY)
    dma = pltpu.SemaphoreType.DMA
    return pl.pallas_call(
        functools.partial(finish_kernel, per),
        in_specs=[anywhere] * 3,
        out_specs=[anywhere] * 4,
        out_shape=[
            jax.ShapeDtypeStruct((NSRC, bins), f32),
            jax.ShapeDtypeStruct((NRCV, bins), f32),
            jax.ShapeDtypeStruct((NOFF, bins), f32),
            jax.ShapeDtypeStruct((1, 1, traces_n, bins), f32),
        ],
        scratch_shapes=[
            pltpu.VMEM(hot.shape, hot.dtype),
            pltpu.VMEM(spectra.shape, f32),
            pltpu.VMEM(turned.shape, f32),
            pltpu.VMEM((ROWS, bins), f32),
            dma((1,)), dma((chunks,)), dma((chunks,)), dma((chunks,)), dma((3,)),
        ],
        compiler_params=pltpu.CompilerParams(vmem_limit_bytes=60 * 1024 * 1024),
    )(hot, spectra, turned)


def on_device(
    nj, ny, nz, traces, source_ids, receiver_ids, offset_ids, receiver_init, offset_init
):
    src, rcv, off = source_ids[0], receiver_ids[0], offset_ids[0]
    spectra, turned, hot = sweep(
        traces[0, 0], src, rcv, off, receiver_init, offset_init, nj, ny, nz
    )
    return finish(hot, spectra, turned.reshape(-1, ROWS), turned.shape[2])


def solution(mesh):
    nsrc, nj = mesh.shape["src"], mesh.shape["rcv"]
    nz = 4 if nsrc >= 32 else 2
    ny = nsrc // nz
    placed = (
        P("src", "rcv", None, None),
        P("src", "rcv", None),
        P("src", "rcv", None),
        P("src", "rcv", None),
        P("rcv", None),
        P(),
    )
    return jax.shard_map(
        functools.partial(on_device, nj, ny, nz),
        mesh=mesh,
        in_specs=placed,
        out_specs=(P("src", None), P("rcv", None), P(), P("src", "rcv", None, None)),
        check_vma=False,
    )
```

```python
import functools

import jax
import jax.numpy as jnp
import ml_dtypes
import numpy as np
from jax import lax
from jax.experimental import pallas as pl
from jax.experimental.pallas import tpu as pltpu
from jax.sharding import PartitionSpec as P

NSRC = 32
NRCV = 32
NOFF = 64
ROWS = NSRC + NRCV + NOFF
MESH = pl.DeviceIdType.MESH
OVER_LANES = (((1,), (1,)), ((), ()))


def dft_tables(samples, bins, chunks):
    times = np.arange(samples, dtype=np.int64)[:, None]
    freqs = np.arange(bins, dtype=np.int64)[None, :]
    phase = (times * freqs) % samples
    angle = phase.astype(np.float32) * np.float32(2.0 * 3.141592653589793 / samples)
    cosine = np.cos(angle).astype(ml_dtypes.bfloat16)
    sine = (-np.sin(angle)).astype(ml_dtypes.bfloat16)
    width = bins // chunks
    return np.stack(
        [
            np.concatenate([t[:, c * width : (c + 1) * width] for t in (cosine, sine)], axis=1)
            for c in range(chunks)
        ]
    )


def hot_rows(src, rcv, off):
    parts = []
    for ids, count in ((src, NSRC), (rcv, NRCV), (off, NOFF)):
        rows = lax.broadcasted_iota(jnp.int32, (count, ids.shape[1]), 0)
        parts.append((rows == ids).astype(jnp.float32))
    return jnp.concatenate(parts, axis=0)


def split(values):
    high = values.astype(jnp.bfloat16)
    low = (values - high.astype(jnp.float32)).astype(jnp.bfloat16)
    return high, low


def dot(a, b):
    return jnp.dot(a, b, preferred_element_type=jnp.float32)


def tiles_of(values, count):
    return [values[:, t * ROWS : (t + 1) * ROWS] for t in range(count)]


def pick(tiles, lane):
    out = pltpu.roll(tiles[0], ROWS - 32, 1)
    out = jnp.where(lane < 32, out, tiles[1])
    out = jnp.where(lane < 64, out, pltpu.roll(tiles[2], 32, 1))
    return jnp.where(lane < 96, out, pltpu.roll(tiles[3], 64, 1))


HALVES = 2


def add(values):
    return functools.reduce(lambda a, b: a + b, values)


def sweep_kernel(
    nj, ny, nz, groups,
    traces_hbm, tables_hbm, src_hbm, rcv_hbm, off_hbm, rinit_hbm, oinit_hbm,
    spectra_hbm, terms_hbm, hot_hbm,
    traces_buf, tables_buf, ids_buf, init_buf, shift_buf, x_buf, hot_buf, sums_buf,
    gs_buf, gy_buf, gz_buf, gr_buf, a_buf, flat_buf, p_buf, b1_buf, b2_buf, t_buf, c_buf, d_out,
    load_sem, table_sem, store_sem, send_sem, recv_sem,
):
    i = lax.axis_index("src")
    j = lax.axis_index("rcv")
    y = i // nz
    z = lax.rem(i, nz)
    samples = traces_buf.shape[1]
    width = x_buf.shape[2]
    per = a_buf.shape[2]
    few = per // ny
    tiles = nj * NRCV // ROWS
    each = nj // groups
    first = j // each

    loads = [
        pltpu.make_async_copy(src_hbm, ids_buf.at[0], load_sem.at[0]),
        pltpu.make_async_copy(rcv_hbm, ids_buf.at[1], load_sem.at[1]),
        pltpu.make_async_copy(off_hbm, ids_buf.at[2], load_sem.at[2]),
        pltpu.make_async_copy(traces_hbm, traces_buf, load_sem.at[3]),
        pltpu.make_async_copy(rinit_hbm, init_buf.at[pl.ds(NSRC, NRCV)], load_sem.at[4]),
        pltpu.make_async_copy(oinit_hbm, init_buf.at[pl.ds(NSRC + NRCV, NOFF)], load_sem.at[5]),
    ]
    order = [h * groups + lax.rem(first + k, groups) for h in range(HALVES) for k in range(groups)]
    tables = [
        pltpu.make_async_copy(tables_hbm.at[c], tables_buf.at[c], table_sem.at[k])
        for k, c in enumerate(order)
    ]
    for copy in loads[:4] + tables[:1] + loads[4:] + tables[1:]:
        copy.start()

    def over_j(d):
        peer = lax.rem(j + d, nj)
        return peer, (i, peer)

    def over_y(d):
        peer = lax.rem(y + d, ny)
        return peer, (peer * nz + z, j)

    def over_z(d):
        peer = lax.rem(z + d, nz)
        return peer, (y * nz + peer, j)

    def copy_to(device, source, target, phase):
        return pltpu.make_async_remote_copy(
            src_ref=source, dst_ref=target, send_sem=send_sem.at[phase],
            recv_sem=recv_sem.at[phase], device_id=device, device_id_type=MESH,
        )

    def send(n, over, me, source, buf, phase):
        for d in range(1, n):
            peer, device = over(d)
            copy_to(device, source(peer), buf.at[me], phase).start()

    def all_of(n, over, buf, phase):
        part = buf.at[pl.ds(0, n - 1)]
        return copy_to(over(1)[1], part, part, phase)

    barrier = pltpu.get_barrier_semaphore()
    for n, over in ((ny, over_y), (nj, over_j), (nz, over_z)):
        for d in range(1, n):
            pl.semaphore_signal(barrier, inc=1, device_id=over(d)[1], device_id_type=MESH)

    for copy in loads[:3]:
        copy.wait()
    hot = hot_rows(ids_buf[0], ids_buf[1], ids_buf[2])
    hot_buf[...] = hot.T.astype(jnp.bfloat16)
    hot = hot.astype(jnp.bfloat16)
    gram = lax.dot_general(hot, hot, OVER_LANES, preferred_element_type=jnp.float32)
    gs_buf[j] = gram[:NSRC]
    gy_buf[y] = gram[NSRC : NSRC + NRCV]
    row = lax.broadcasted_iota(jnp.int32, (ROWS, ROWS), 0)
    lane = lax.broadcasted_iota(jnp.int32, (ROWS, ROWS), 1)
    from_rcv = (lane >= NSRC) & (lane < NSRC + NRCV) & (row < NSRC)
    from_off = (lane >= NSRC + NRCV) & (row < NSRC + NRCV)
    before = jnp.where(from_rcv | from_off, gram, 0.0).astype(jnp.bfloat16)
    pl.semaphore_wait(barrier, nj + ny + nz - 3)
    send(nj, over_j, j, lambda p: gs_buf.at[j], gs_buf, 0)
    stores = [pltpu.make_async_copy(hot_buf, hot_hbm, load_sem.at[0])]
    stores[0].start()

    for copy in loads[4:]:
        copy.wait()
    init_buf[:NSRC] = jnp.zeros((NSRC, init_buf.shape[1]), jnp.float32)
    shift_buf[...] = dot(
        jnp.concatenate([before, before], axis=1), jnp.concatenate(split(init_buf[...]), axis=0)
    )
    loads[3].wait()
    for n, c in enumerate(order):
        h, k = n // groups, n % groups
        g = c - h * groups
        tables[n].wait()
        both = dot(traces_buf[...], tables_buf[c])
        real, imag = both[:, :width], both[:, width:]
        spectra = 0.5 * jnp.log((real * real + imag * imag) * (1.0 / samples) + 0.25)
        x_buf[c] = spectra
        store = pltpu.make_async_copy(x_buf.at[c], spectra_hbm.at[c], store_sem.at[n])
        store.start()
        stores.append(store)
        spec_high, spec_low = split(spectra)
        span = pl.ds(pl.multiple_of(c * width, width), width)
        sums = dot(hot, spec_high) + dot(hot, spec_low) - shift_buf[:, span]
        turned = sums.T
        for q in range(each):
            sums_buf[h, g * each + q] = turned[q * per : (q + 1) * per]
        for q in range(1 if k == 0 else 0, each):
            peer = g * each + (lax.rem(j + q, each) if k == 0 else q)
            copy_to((i, peer), sums_buf.at[h, peer], a_buf.at[h, j], 4 + 5 * h).start()
        if n == groups - 1:
            send(ny, over_y, y, lambda p: gy_buf.at[y], gy_buf, 1)
    for h in range(HALVES):
        a_buf[h, j] = sums_buf[h, j]

    all_of(nj, over_j, gs_buf, 0).wait_recv()
    by_src = [gs_buf[q] for q in range(nj)]
    src_count = add(by_src)
    n_src = jnp.sum(src_count, axis=0, keepdims=True) + 1.0
    off_high, off_low = split(src_count)
    counts = [
        pick(by_src[4 * t : 4 * t + 4], lane[:NSRC]).astype(jnp.bfloat16) for t in range(tiles)
    ]
    counts = jnp.concatenate(counts + [off_high, off_low], axis=1)
    lane = lane[:per]
    all_of(ny, over_y, gy_buf, 1).wait_recv()
    gz_buf[z] = jnp.sum(gy_buf[...], axis=0)
    send(nz, over_z, z, lambda p: gz_buf.at[z], gz_buf, 2)

    def source_step(h):
        all_of(nj, over_j, a_buf.at[h], 4 + 5 * h).wait_recv()
        parts = [a_buf[h, q] for q in range(nj)]
        total = add(parts)
        src_terms = jnp.where(lane < NSRC, total / n_src, 0.0)
        both = dot(jnp.concatenate(split(src_terms[:, :NSRC]), axis=0), counts)
        along = tiles_of(both[:per] + both[per:], tiles + 2)
        for t in range(tiles):
            left = pick(parts[4 * t : 4 * t + 4], lane) - along[t]
            flat_buf[h, :, t * ROWS : (t + 1) * ROWS] = left
        flat_buf[h, :, tiles * ROWS :] = total - along[tiles] - along[tiles + 1]
        for q in range(ny):
            p_buf[h, q] = flat_buf[h, q * few : (q + 1) * few, :]
        send(ny, over_y, y, lambda p: p_buf.at[h, p], b1_buf.at[h], 5 + 5 * h)
        b1_buf[h, y] = p_buf[h, y]
        return src_terms

    def reduce_step(h):
        all_of(ny, over_y, b1_buf.at[h], 5 + 5 * h).wait_recv()
        b2_buf[h, z] = add([b1_buf[h, q] for q in range(ny)])
        send(nz, over_z, z, lambda p: b2_buf.at[h, z], b2_buf.at[h], 6 + 5 * h)

    def term_step(h):
        all_of(nz, over_z, b2_buf.at[h], 6 + 5 * h).wait_recv()
        reduced = add([b2_buf[h, q] for q in range(nz)])
        rcv_terms = reduced[:, : tiles * ROWS] / n_rcv
        for k, part in enumerate(split(rcv_terms)):
            t_buf[h, k * few : (k + 1) * few, :] = part.astype(jnp.float32)
        both = dot(t_buf[h].astype(jnp.bfloat16), by_rcv)
        both = both[:few] + both[few:]
        later = reduced[:, tiles * ROWS :] - both[:, :ROWS] - both[:, ROWS:]
        c_buf[h, y] = jnp.concatenate([rcv_terms, later / n_off], axis=1)
        send(ny, over_y, y, lambda p: c_buf.at[h, y], c_buf.at[h], 7 + 5 * h)

    def back_step(h, src_terms):
        all_of(ny, over_y, c_buf.at[h], 7 + 5 * h).wait_recv()
        for q in range(ny):
            flat_buf[h, q * few : (q + 1) * few, :] = c_buf[h, q]
        off_tile = flat_buf[h, :, tiles * ROWS :]
        for t in range(tiles):
            tile = flat_buf[h, :, t * ROWS : (t + 1) * ROWS]
            for q in range(4):
                turned = tile if q == 1 else pltpu.roll(tile, (32 - 32 * q) % ROWS, 1)
                d_out[h, 4 * t + q] = jnp.where(
                    lane < NSRC, src_terms, jnp.where(lane < NSRC + NRCV, turned, off_tile)
                )
        send(nj, over_j, j, lambda p: d_out.at[h, p], terms_hbm.at[h], 8 + 5 * h)
        own = pltpu.make_async_copy(d_out.at[h, j], terms_hbm.at[h, j], load_sem.at[1 + h])
        own.start()
        stores.append(own)

    src_low = source_step(0)
    src_high = source_step(1)
    all_of(nz, over_z, gz_buf, 2).wait_recv()
    count = jnp.sum(gz_buf[...], axis=0)
    half = NRCV // 2
    wide = lax.broadcasted_iota(jnp.int32, (half, ROWS), 1) >= NSRC + NRCV
    gr_buf[j] = jnp.where(wide, count[:half], pltpu.roll(count[half:], ROWS // 2, 1))
    send(nj, over_j, j, lambda p: gr_buf.at[j], gr_buf, 3)
    reduce_step(0)
    reduce_step(1)

    all_of(nj, over_j, gr_buf, 3).wait_recv()
    by_rcv = []
    for q in range(nj):
        packed = gr_buf[q]
        by_rcv.append(jnp.where(wide, packed, 0.0))
        by_rcv.append(jnp.where(wide, pltpu.roll(packed, ROWS // 2, 1), 0.0))
    by_rcv = jnp.concatenate(by_rcv, axis=0)
    n_off = jnp.sum(by_rcv, axis=0, keepdims=True) + 1.0
    by_rcv = split(by_rcv)
    ones = jnp.ones((16, ROWS), jnp.bfloat16)
    n_rcv = add(
        [
            lax.dot_general(ones, part, OVER_LANES, preferred_element_type=jnp.float32)
            for part in by_rcv
        ]
    )[:1] + 1.0
    by_rcv = jnp.concatenate(by_rcv, axis=1)

    term_step(0)
    term_step(1)
    back_step(0, src_low)
    back_step(1, src_high)

    for phase, (n, over, buf) in enumerate(
        [(nj, over_j, gs_buf), (ny, over_y, gy_buf), (nz, over_z, gz_buf), (nj, over_j, gr_buf)]
    ):
        all_of(n, over, buf, phase).wait_send()
    for h in range(HALVES):
        for phase, (n, over, buf) in enumerate(
            [
                (nj, over_j, a_buf), (ny, over_y, b1_buf), (nz, over_z, b2_buf),
                (ny, over_y, c_buf), (nj, over_j, d_out),
            ]
        ):
            all_of(n, over, buf.at[h], 4 + 5 * h + phase).wait_send()
    for store in stores:
        store.wait()
    for h in range(HALVES):
        all_of(nj, over_j, terms_hbm.at[h], 8 + 5 * h).wait_recv()


def sweep(traces, src, rcv, off, receiver_init, offset_init, nj, ny, nz):
    traces_n, samples = traces.shape
    bins = receiver_init.shape[1]
    groups = max(1, bins // (256 * HALVES))
    chunks = HALVES * groups
    width = bins // chunks
    per = bins // nj // HALVES
    few = per // ny
    wide = nj * NRCV + ROWS
    f32, b16 = jnp.float32, jnp.bfloat16
    tables = jnp.asarray(dft_tables(samples, bins, chunks))
    anywhere = pl.BlockSpec(memory_space=pl.ANY)
    dma = pltpu.SemaphoreType.DMA
    phases = 4 + 5 * HALVES
    return pl.pallas_call(
        functools.partial(sweep_kernel, nj, ny, nz, groups),
        in_specs=[anywhere] * 7,
        out_specs=[anywhere] * 3,
        out_shape=[
            jax.ShapeDtypeStruct((chunks, traces_n, width), f32),
            jax.ShapeDtypeStruct((HALVES, nj, per, ROWS), f32),
            jax.ShapeDtypeStruct((traces_n, ROWS), b16),
        ],
        scratch_shapes=[
            pltpu.VMEM((traces_n, samples), b16),
            pltpu.VMEM((chunks, samples, 2 * width), b16),
            pltpu.VMEM((3, 1, traces_n), jnp.int32),
            pltpu.VMEM((ROWS, bins), f32),
            pltpu.VMEM((ROWS, bins), f32),
            pltpu.VMEM((chunks, traces_n, width), f32),
            pltpu.VMEM((traces_n, ROWS), b16),
            pltpu.VMEM((HALVES, nj, per, ROWS), f32),
            pltpu.VMEM((nj, NSRC, ROWS), f32),
            pltpu.VMEM((ny, NRCV, ROWS), f32),
            pltpu.VMEM((nz, NRCV, ROWS), f32),
            pltpu.VMEM((nj, NRCV // 2, ROWS), f32),
            pltpu.VMEM((HALVES, nj, per, ROWS), f32),
            pltpu.VMEM((HALVES, per, wide), f32),
            pltpu.VMEM((HALVES, ny, few, wide), f32),
            pltpu.VMEM((HALVES, ny, few, wide), f32),
            pltpu.VMEM((HALVES, nz, few, wide), f32),
            pltpu.VMEM((HALVES, 2 * few, nj * NRCV), f32),
            pltpu.VMEM((HALVES, ny, few, wide), f32),
            pltpu.VMEM((HALVES, nj, per, ROWS), f32),
            dma((6,)), dma((chunks,)), dma((chunks,)), dma((phases,)), dma((phases,)),
        ],
        compiler_params=pltpu.CompilerParams(
            collective_id=0, has_side_effects=True, vmem_limit_bytes=60 * 1024 * 1024
        ),
    )(traces, tables, src, rcv, off, receiver_init, offset_init)


def finish_kernel(
    hot_hbm, spectra_hbm, turned_hbm, src_out, rcv_out, off_out, residual_out,
    hot_buf, x_buf, turned_buf, terms_buf, load_sem, x_sem, turned_sem, store_sem, out_sem,
):
    chunks, _, width = x_buf.shape
    load = pltpu.make_async_copy(hot_hbm, hot_buf, load_sem.at[0])
    load.start()
    parts = []
    for c in range(chunks):
        rows = pl.ds(c * width, width)
        parts.append((
            pltpu.make_async_copy(turned_hbm.at[rows], turned_buf.at[rows], turned_sem.at[c]),
            pltpu.make_async_copy(spectra_hbm.at[c], x_buf.at[c], x_sem.at[c]),
        ))
        for copy in parts[c]:
            copy.start()
    load.wait()
    hot = jnp.concatenate([hot_buf[...]] * 2, axis=1)
    stores = []
    for c in range(chunks):
        for copy in parts[c]:
            copy.wait()
        span = slice(c * width, (c + 1) * width)
        turned = turned_buf[span]
        both = jnp.concatenate(split(turned), axis=1)
        spread = lax.dot_general(hot, both, OVER_LANES, preferred_element_type=jnp.float32)
        x_buf[c] = x_buf[c] - spread
        store = pltpu.make_async_copy(
            x_buf.at[c], residual_out.at[0, 0, :, pl.ds(c * width, width)], store_sem.at[c]
        )
        store.start()
        stores.append(store)
        terms_buf[:, span] = turned.T
    start = 0
    for k, (out, count) in enumerate(((src_out, NSRC), (rcv_out, NRCV), (off_out, NOFF))):
        store = pltpu.make_async_copy(terms_buf.at[pl.ds(start, count)], out, out_sem.at[k])
        store.start()
        stores.append(store)
        start += count
    for store in stores:
        store.wait()


def finish(hot, spectra, turned):
    chunks, traces_n, width = spectra.shape
    bins = chunks * width
    f32 = jnp.float32
    anywhere = pl.BlockSpec(memory_space=pl.ANY)
    dma = pltpu.SemaphoreType.DMA
    return pl.pallas_call(
        finish_kernel,
        in_specs=[anywhere] * 3,
        out_specs=[anywhere] * 4,
        out_shape=[
            jax.ShapeDtypeStruct((NSRC, bins), f32),
            jax.ShapeDtypeStruct((NRCV, bins), f32),
            jax.ShapeDtypeStruct((NOFF, bins), f32),
            jax.ShapeDtypeStruct((1, 1, traces_n, bins), f32),
        ],
        scratch_shapes=[
            pltpu.VMEM(hot.shape, hot.dtype),
            pltpu.VMEM(spectra.shape, f32),
            pltpu.VMEM(turned.shape, f32),
            pltpu.VMEM((ROWS, bins), f32),
            dma((1,)), dma((chunks,)), dma((chunks,)), dma((chunks,)), dma((3,)),
        ],
        compiler_params=pltpu.CompilerParams(vmem_limit_bytes=60 * 1024 * 1024),
    )(hot, spectra, turned)


def on_device(
    nj, ny, nz, traces, source_ids, receiver_ids, offset_ids, receiver_init, offset_init
):
    src, rcv, off = source_ids[0], receiver_ids[0], offset_ids[0]
    spectra, turned, hot = sweep(
        traces[0, 0], src, rcv, off, receiver_init, offset_init, nj, ny, nz
    )
    return finish(hot, spectra, turned.reshape(-1, ROWS))


def solution(mesh):
    nsrc, nj = mesh.shape["src"], mesh.shape["rcv"]
    nz = 4 if nsrc >= 32 else 2
    ny = nsrc // nz
    placed = (
        P("src", "rcv", None, None),
        P("src", "rcv", None),
        P("src", "rcv", None),
        P("src", "rcv", None),
        P("rcv", None),
        P(),
    )
    return jax.shard_map(
        functools.partial(on_device, nj, ny, nz),
        mesh=mesh,
        in_specs=placed,
        out_specs=(P("src", None), P("rcv", None), P(), P("src", "rcv", None, None)),
        check_vma=False,
    )
```

```python
import functools

import jax
import jax.numpy as jnp
import ml_dtypes
import numpy as np
from jax import lax
from jax.experimental import pallas as pl
from jax.experimental.pallas import tpu as pltpu
from jax.sharding import PartitionSpec as P

NSRC = 32
NRCV = 32
NOFF = 64
ROWS = NSRC + NRCV + NOFF
MESH = pl.DeviceIdType.MESH
OVER_LANES = (((1,), (1,)), ((), ()))


def dft_tables(samples, bins, chunks):
    times = np.arange(samples, dtype=np.int64)[:, None]
    freqs = np.arange(bins, dtype=np.int64)[None, :]
    phase = (times * freqs) % samples
    angle = phase.astype(np.float32) * np.float32(2.0 * 3.141592653589793 / samples)
    cosine = np.cos(angle).astype(ml_dtypes.bfloat16)
    sine = (-np.sin(angle)).astype(ml_dtypes.bfloat16)
    width = bins // chunks
    return np.stack(
        [
            np.concatenate([t[:, c * width : (c + 1) * width] for t in (cosine, sine)], axis=1)
            for c in range(chunks)
        ]
    )


def hot_rows(src, rcv, off):
    parts = []
    for ids, count in ((src, NSRC), (rcv, NRCV), (off, NOFF)):
        rows = lax.broadcasted_iota(jnp.int32, (count, ids.shape[1]), 0)
        parts.append((rows == ids).astype(jnp.float32))
    return jnp.concatenate(parts, axis=0)


def split(values):
    high = values.astype(jnp.bfloat16)
    low = (values - high.astype(jnp.float32)).astype(jnp.bfloat16)
    return high, low


def dot(a, b):
    return jnp.dot(a, b, preferred_element_type=jnp.float32)


def tiles_of(values, count):
    return [values[:, t * ROWS : (t + 1) * ROWS] for t in range(count)]


def pick(tiles, lane):
    out = pltpu.roll(tiles[0], ROWS - 32, 1)
    out = jnp.where(lane < 32, out, tiles[1])
    out = jnp.where(lane < 64, out, pltpu.roll(tiles[2], 32, 1))
    return jnp.where(lane < 96, out, pltpu.roll(tiles[3], 64, 1))


HALVES = 2


def add(values):
    return functools.reduce(lambda a, b: a + b, values)


def sweep_kernel(
    nj, ny, nz, groups,
    traces_hbm, tables_hbm, src_hbm, rcv_hbm, off_hbm, rinit_hbm, oinit_hbm,
    spectra_hbm, terms_hbm, hot_hbm,
    traces_buf, tables_buf, ids_buf, init_buf, shift_buf, x_buf, hot_buf, sums_buf,
    gs_buf, gy_buf, gz_buf, gr_buf, a_buf, flat_buf, p_buf, b1_buf, b2_buf, t_buf, c_buf, d_out, d_buf, f_out,
    load_sem, table_sem, store_sem, send_sem, recv_sem,
):
    i = lax.axis_index("src")
    j = lax.axis_index("rcv")
    y = i // nz
    z = lax.rem(i, nz)
    samples = traces_buf.shape[1]
    width = x_buf.shape[2]
    per = a_buf.shape[2]
    few = per // ny
    quarter = per // 4
    tiles = nj * NRCV // ROWS
    chips = nj // 2
    chip = j // 2
    core = lax.rem(j, 2)
    partner = (i, j + 1 - 2 * core)
    each = nj // groups
    first = j // each

    loads = [
        pltpu.make_async_copy(src_hbm, ids_buf.at[0], load_sem.at[0]),
        pltpu.make_async_copy(rcv_hbm, ids_buf.at[1], load_sem.at[1]),
        pltpu.make_async_copy(off_hbm, ids_buf.at[2], load_sem.at[2]),
        pltpu.make_async_copy(traces_hbm, traces_buf, load_sem.at[3]),
        pltpu.make_async_copy(rinit_hbm, init_buf.at[pl.ds(NSRC, NRCV)], load_sem.at[4]),
        pltpu.make_async_copy(oinit_hbm, init_buf.at[pl.ds(NSRC + NRCV, NOFF)], load_sem.at[5]),
    ]
    order = [h * groups + lax.rem(first + k, groups) for h in range(HALVES) for k in range(groups)]
    tables = [
        pltpu.make_async_copy(tables_hbm.at[c], tables_buf.at[c], table_sem.at[k])
        for k, c in enumerate(order)
    ]
    for copy in loads[:4] + tables[:1] + loads[4:] + tables[1:]:
        copy.start()

    def over_j(d):
        peer = lax.rem(j + d, nj)
        return peer, (i, peer)

    def over_y(d):
        peer = lax.rem(y + d, ny)
        return peer, (peer * nz + z, j)

    def over_z(d):
        peer = lax.rem(z + d, nz)
        return peer, (y * nz + peer, j)

    def over_chips(d):
        peer = lax.rem(chip + d, chips)
        return peer, (i, 2 * peer + core)

    def copy_to(device, source, target, phase):
        return pltpu.make_async_remote_copy(
            src_ref=source, dst_ref=target, send_sem=send_sem.at[phase],
            recv_sem=recv_sem.at[phase], device_id=device, device_id_type=MESH,
        )

    def send(n, over, me, source, buf, phase):
        for d in range(1, n):
            peer, device = over(d)
            copy_to(device, source(peer), buf.at[me], phase).start()

    def all_of(n, over, buf, phase):
        part = buf.at[pl.ds(0, n - 1)]
        return copy_to(over(1)[1], part, part, phase)

    barrier = pltpu.get_barrier_semaphore()
    for n, over in ((ny, over_y), (nj, over_j), (nz, over_z)):
        for d in range(1, n):
            pl.semaphore_signal(barrier, inc=1, device_id=over(d)[1], device_id_type=MESH)

    for copy in loads[:3]:
        copy.wait()
    hot = hot_rows(ids_buf[0], ids_buf[1], ids_buf[2])
    hot_buf[...] = hot.T.astype(jnp.bfloat16)
    hot = hot.astype(jnp.bfloat16)
    gram = lax.dot_general(hot, hot, OVER_LANES, preferred_element_type=jnp.float32)
    gs_buf[j] = gram[:NSRC]
    gy_buf[y] = gram[NSRC : NSRC + NRCV]
    row = lax.broadcasted_iota(jnp.int32, (ROWS, ROWS), 0)
    lane = lax.broadcasted_iota(jnp.int32, (ROWS, ROWS), 1)
    from_rcv = (lane >= NSRC) & (lane < NSRC + NRCV) & (row < NSRC)
    from_off = (lane >= NSRC + NRCV) & (row < NSRC + NRCV)
    before = jnp.where(from_rcv | from_off, gram, 0.0).astype(jnp.bfloat16)
    pl.semaphore_wait(barrier, nj + ny + nz - 3)
    send(nj, over_j, j, lambda p: gs_buf.at[j], gs_buf, 0)
    stores = [pltpu.make_async_copy(hot_buf, hot_hbm, load_sem.at[0])]
    stores[0].start()

    for copy in loads[4:]:
        copy.wait()
    init_buf[:NSRC] = jnp.zeros((NSRC, init_buf.shape[1]), jnp.float32)
    shift_buf[...] = dot(
        jnp.concatenate([before, before], axis=1), jnp.concatenate(split(init_buf[...]), axis=0)
    )
    loads[3].wait()
    for n, c in enumerate(order):
        h, k = n // groups, n % groups
        g = c - h * groups
        tables[n].wait()
        both = dot(traces_buf[...], tables_buf[c])
        real, imag = both[:, :width], both[:, width:]
        spectra = 0.5 * jnp.log((real * real + imag * imag) * (1.0 / samples) + 0.25)
        x_buf[c] = spectra
        store = pltpu.make_async_copy(x_buf.at[c], spectra_hbm.at[c], store_sem.at[n])
        store.start()
        stores.append(store)
        spec_high, spec_low = split(spectra)
        span = pl.ds(pl.multiple_of(c * width, width), width)
        sums = dot(hot, spec_high) + dot(hot, spec_low) - shift_buf[:, span]
        turned = sums.T
        for q in range(each):
            sums_buf[h, g * each + q] = turned[q * per : (q + 1) * per]
        for q in range(1 if k == 0 else 0, each):
            peer = g * each + (lax.rem(j + q, each) if k == 0 else q)
            copy_to((i, peer), sums_buf.at[h, peer], a_buf.at[h, j], 4 + 5 * h).start()
        if n == groups - 1:
            send(ny, over_y, y, lambda p: gy_buf.at[y], gy_buf, 1)
    for h in range(HALVES):
        a_buf[h, j] = sums_buf[h, j]

    all_of(nj, over_j, gs_buf, 0).wait_recv()
    by_src = [gs_buf[q] for q in range(nj)]
    src_count = add(by_src)
    n_src = jnp.sum(src_count, axis=0, keepdims=True) + 1.0
    off_high, off_low = split(src_count)
    counts = [
        pick(by_src[4 * t : 4 * t + 4], lane[:NSRC]).astype(jnp.bfloat16) for t in range(tiles)
    ]
    counts = jnp.concatenate(counts + [off_high, off_low], axis=1)
    lane = lane[:per]
    all_of(ny, over_y, gy_buf, 1).wait_recv()
    gz_buf[z] = jnp.sum(gy_buf[...], axis=0)
    send(nz, over_z, z, lambda p: gz_buf.at[z], gz_buf, 2)

    def source_step(h):
        all_of(nj, over_j, a_buf.at[h], 4 + 5 * h).wait_recv()
        parts = [a_buf[h, q] for q in range(nj)]
        total = add(parts)
        src_terms = jnp.where(lane < NSRC, total / n_src, 0.0)
        both = dot(jnp.concatenate(split(src_terms[:, :NSRC]), axis=0), counts)
        along = tiles_of(both[:per] + both[per:], tiles + 2)
        for t in range(tiles):
            left = pick(parts[4 * t : 4 * t + 4], lane) - along[t]
            flat_buf[h, :, t * ROWS : (t + 1) * ROWS] = left
        flat_buf[h, :, tiles * ROWS :] = total - along[tiles] - along[tiles + 1]
        for q in range(ny):
            p_buf[h, q] = flat_buf[h, q * few : (q + 1) * few, :]
        send(ny, over_y, y, lambda p: p_buf.at[h, p], b1_buf.at[h], 5 + 5 * h)
        b1_buf[h, y] = p_buf[h, y]
        return src_terms

    def reduce_step(h):
        all_of(ny, over_y, b1_buf.at[h], 5 + 5 * h).wait_recv()
        b2_buf[h, z] = add([b1_buf[h, q] for q in range(ny)])
        send(nz, over_z, z, lambda p: b2_buf.at[h, z], b2_buf.at[h], 6 + 5 * h)

    def term_step(h):
        all_of(nz, over_z, b2_buf.at[h], 6 + 5 * h).wait_recv()
        reduced = add([b2_buf[h, q] for q in range(nz)])
        rcv_terms = reduced[:, : tiles * ROWS] / n_rcv
        for k, part in enumerate(split(rcv_terms)):
            t_buf[h, k * few : (k + 1) * few, :] = part.astype(jnp.float32)
        both = dot(t_buf[h].astype(jnp.bfloat16), by_rcv)
        both = both[:few] + both[few:]
        later = reduced[:, tiles * ROWS :] - both[:, :ROWS] - both[:, ROWS:]
        c_buf[h, y] = jnp.concatenate([rcv_terms, later / n_off], axis=1)
        send(ny, over_y, y, lambda p: c_buf.at[h, y], c_buf.at[h], 7 + 5 * h)

    def back_step(h, src_terms):
        all_of(ny, over_y, c_buf.at[h], 7 + 5 * h).wait_recv()
        for q in range(ny):
            flat_buf[h, q * few : (q + 1) * few, :] = c_buf[h, q]
        off_tile = flat_buf[h, :, tiles * ROWS :]
        for t in range(tiles):
            tile = flat_buf[h, :, t * ROWS : (t + 1) * ROWS]
            for k in range(2):
                zero = pltpu.roll(tile, (32 - 64 * k) % ROWS, 1)
                one = pltpu.roll(tile, (-64 * k) % ROWS, 1) if k else tile
                same = jnp.where(is_zero, zero, one)
                other = jnp.where(is_zero, one, zero)
                d_out[h, 2 * t + k, :per, :] = jnp.where(
                    lane < NSRC, src_terms, jnp.where(lane < NSRC + NRCV, same, off_tile)
                )
                parts = [other[q * quarter : (q + 1) * quarter] for q in range(4)]
                d_out[h, 2 * t + k, per:, :] = pick(parts, lane[:quarter])
        send(chips, over_chips, chip, lambda p: d_out.at[h, p], d_buf.at[h], 8 + 5 * h)
        d_buf[h, chip] = d_out[h, chip]

    def pair_copy(h, place):
        return copy_to(partner, f_out.at[h], terms_hbm.at[h, place], 4 + 5 * HALVES + h)

    def pair_step(h):
        all_of(chips, over_chips, d_buf.at[h], 8 + 5 * h).wait_recv()
        own = pltpu.make_async_copy(
            d_buf.at[h, :, pl.ds(0, per)], terms_hbm.at[h, core], load_sem.at[1 + h]
        )
        own.start()
        stores.append(own)
        inside = (lane[:quarter] >= NSRC) & (lane[:quarter] < NSRC + NRCV)
        for p in range(chips):
            packed = d_buf[h, p, per:, :]
            for q in range(4):
                rows = slice(q * quarter, (q + 1) * quarter)
                other = packed if q == 1 else pltpu.roll(packed, (32 - 32 * q) % ROWS, 1)
                f_out[h, p, rows, :] = jnp.where(inside, other, d_buf[h, p, rows, :])
        pair_copy(h, core).start()

    is_zero = jnp.zeros((per, ROWS), jnp.int32) + core == 0
    src_low = source_step(0)
    src_high = source_step(1)
    all_of(nz, over_z, gz_buf, 2).wait_recv()
    count = jnp.sum(gz_buf[...], axis=0)
    half = NRCV // 2
    wide = lax.broadcasted_iota(jnp.int32, (half, ROWS), 1) >= NSRC + NRCV
    gr_buf[j] = jnp.where(wide, count[:half], pltpu.roll(count[half:], ROWS // 2, 1))
    send(nj, over_j, j, lambda p: gr_buf.at[j], gr_buf, 3)
    reduce_step(0)
    reduce_step(1)

    all_of(nj, over_j, gr_buf, 3).wait_recv()
    by_rcv = []
    for q in range(nj):
        packed = gr_buf[q]
        by_rcv.append(jnp.where(wide, packed, 0.0))
        by_rcv.append(jnp.where(wide, pltpu.roll(packed, ROWS // 2, 1), 0.0))
    by_rcv = jnp.concatenate(by_rcv, axis=0)
    n_off = jnp.sum(by_rcv, axis=0, keepdims=True) + 1.0
    by_rcv = split(by_rcv)
    ones = jnp.ones((16, ROWS), jnp.bfloat16)
    n_rcv = add(
        [
            lax.dot_general(ones, part, OVER_LANES, preferred_element_type=jnp.float32)
            for part in by_rcv
        ]
    )[:1] + 1.0
    by_rcv = jnp.concatenate(by_rcv, axis=1)

    term_step(0)
    term_step(1)
    back_step(0, src_low)
    back_step(1, src_high)
    pair_step(0)
    pair_step(1)

    for phase, (n, over, buf) in enumerate(
        [(nj, over_j, gs_buf), (ny, over_y, gy_buf), (nz, over_z, gz_buf), (nj, over_j, gr_buf)]
    ):
        all_of(n, over, buf, phase).wait_send()
    for h in range(HALVES):
        for phase, (n, over, buf) in enumerate(
            [
                (nj, over_j, a_buf), (ny, over_y, b1_buf), (nz, over_z, b2_buf),
                (ny, over_y, c_buf), (chips, over_chips, d_buf),
            ]
        ):
            all_of(n, over, buf.at[h], 4 + 5 * h + phase).wait_send()
    for store in stores:
        store.wait()
    for h in range(HALVES):
        pair_copy(h, core).wait_send()
        pair_copy(h, 1 - core).wait_recv()


def sweep(traces, src, rcv, off, receiver_init, offset_init, nj, ny, nz):
    traces_n, samples = traces.shape
    bins = receiver_init.shape[1]
    groups = max(1, bins // (256 * HALVES))
    chunks = HALVES * groups
    width = bins // chunks
    per = bins // nj // HALVES
    few = per // ny
    wide = nj * NRCV + ROWS
    f32, b16 = jnp.float32, jnp.bfloat16
    tables = jnp.asarray(dft_tables(samples, bins, chunks))
    anywhere = pl.BlockSpec(memory_space=pl.ANY)
    dma = pltpu.SemaphoreType.DMA
    phases = 4 + 6 * HALVES
    return pl.pallas_call(
        functools.partial(sweep_kernel, nj, ny, nz, groups),
        in_specs=[anywhere] * 7,
        out_specs=[anywhere] * 3,
        out_shape=[
            jax.ShapeDtypeStruct((chunks, traces_n, width), f32),
            jax.ShapeDtypeStruct((HALVES, 2, nj // 2, per, ROWS), f32),
            jax.ShapeDtypeStruct((traces_n, ROWS), b16),
        ],
        scratch_shapes=[
            pltpu.VMEM((traces_n, samples), b16),
            pltpu.VMEM((chunks, samples, 2 * width), b16),
            pltpu.VMEM((3, 1, traces_n), jnp.int32),
            pltpu.VMEM((ROWS, bins), f32),
            pltpu.VMEM((ROWS, bins), f32),
            pltpu.VMEM((chunks, traces_n, width), f32),
            pltpu.VMEM((traces_n, ROWS), b16),
            pltpu.VMEM((HALVES, nj, per, ROWS), f32),
            pltpu.VMEM((nj, NSRC, ROWS), f32),
            pltpu.VMEM((ny, NRCV, ROWS), f32),
            pltpu.VMEM((nz, NRCV, ROWS), f32),
            pltpu.VMEM((nj, NRCV // 2, ROWS), f32),
            pltpu.VMEM((HALVES, nj, per, ROWS), f32),
            pltpu.VMEM((HALVES, per, wide), f32),
            pltpu.VMEM((HALVES, ny, few, wide), f32),
            pltpu.VMEM((HALVES, ny, few, wide), f32),
            pltpu.VMEM((HALVES, nz, few, wide), f32),
            pltpu.VMEM((HALVES, 2 * few, nj * NRCV), f32),
            pltpu.VMEM((HALVES, ny, few, wide), f32),
            pltpu.VMEM((HALVES, nj // 2, per + per // 4, ROWS), f32),
            pltpu.VMEM((HALVES, nj // 2, per + per // 4, ROWS), f32),
            pltpu.VMEM((HALVES, nj // 2, per, ROWS), f32),
            dma((6,)), dma((chunks,)), dma((chunks,)), dma((phases,)), dma((phases,)),
        ],
        compiler_params=pltpu.CompilerParams(
            collective_id=0, has_side_effects=True, vmem_limit_bytes=60 * 1024 * 1024
        ),
    )(traces, tables, src, rcv, off, receiver_init, offset_init)


def finish_kernel(
    hot_hbm, spectra_hbm, turned_hbm, src_out, rcv_out, off_out, residual_out,
    hot_buf, x_buf, turned_buf, terms_buf, load_sem, x_sem, turned_sem, store_sem, out_sem,
):
    chunks, _, width = x_buf.shape
    load = pltpu.make_async_copy(hot_hbm, hot_buf, load_sem.at[0])
    load.start()
    parts = []
    _, cores, taken, _, _ = turned_buf.shape
    groups = chunks // HALVES
    for c in range(chunks):
        source = turned_hbm.at[c // groups, :, pl.ds(c % groups * taken, taken)]
        parts.append((
            pltpu.make_async_copy(source, turned_buf.at[c], turned_sem.at[c]),
            pltpu.make_async_copy(spectra_hbm.at[c], x_buf.at[c], x_sem.at[c]),
        ))
        for copy in parts[c]:
            copy.start()
    load.wait()
    hot = jnp.concatenate([hot_buf[...]] * 2, axis=1)
    stores = []
    for c in range(chunks):
        for copy in parts[c]:
            copy.wait()
        span = slice(c * width, (c + 1) * width)
        turned = jnp.concatenate(
            [turned_buf[c, core, p] for p in range(taken) for core in range(cores)], axis=0
        )
        both = jnp.concatenate(split(turned), axis=1)
        spread = lax.dot_general(hot, both, OVER_LANES, preferred_element_type=jnp.float32)
        x_buf[c] = x_buf[c] - spread
        store = pltpu.make_async_copy(
            x_buf.at[c], residual_out.at[0, 0, :, pl.ds(c * width, width)], store_sem.at[c]
        )
        store.start()
        stores.append(store)
        terms_buf[:, span] = turned.T
    start = 0
    for k, (out, count) in enumerate(((src_out, NSRC), (rcv_out, NRCV), (off_out, NOFF))):
        store = pltpu.make_async_copy(terms_buf.at[pl.ds(start, count)], out, out_sem.at[k])
        store.start()
        stores.append(store)
        start += count
    for store in stores:
        store.wait()


def finish(hot, spectra, turned):
    chunks, traces_n, width = spectra.shape
    bins = chunks * width
    halves, cores, chips, per, rows = turned.shape
    taken = chips * halves // chunks
    f32 = jnp.float32
    anywhere = pl.BlockSpec(memory_space=pl.ANY)
    dma = pltpu.SemaphoreType.DMA
    return pl.pallas_call(
        finish_kernel,
        in_specs=[anywhere] * 3,
        out_specs=[anywhere] * 4,
        out_shape=[
            jax.ShapeDtypeStruct((NSRC, bins), f32),
            jax.ShapeDtypeStruct((NRCV, bins), f32),
            jax.ShapeDtypeStruct((NOFF, bins), f32),
            jax.ShapeDtypeStruct((1, 1, traces_n, bins), f32),
        ],
        scratch_shapes=[
            pltpu.VMEM(hot.shape, hot.dtype),
            pltpu.VMEM(spectra.shape, f32),
            pltpu.VMEM((chunks, cores, taken, per, rows), f32),
            pltpu.VMEM((ROWS, bins), f32),
            dma((1,)), dma((chunks,)), dma((chunks,)), dma((chunks,)), dma((3,)),
        ],
        compiler_params=pltpu.CompilerParams(vmem_limit_bytes=60 * 1024 * 1024),
    )(hot, spectra, turned)


def on_device(
    nj, ny, nz, traces, source_ids, receiver_ids, offset_ids, receiver_init, offset_init
):
    src, rcv, off = source_ids[0], receiver_ids[0], offset_ids[0]
    spectra, turned, hot = sweep(
        traces[0, 0], src, rcv, off, receiver_init, offset_init, nj, ny, nz
    )
    return finish(hot, spectra, turned)


def solution(mesh):
    nsrc, nj = mesh.shape["src"], mesh.shape["rcv"]
    nz = 4 if nsrc >= 32 else 2
    ny = nsrc // nz
    placed = (
        P("src", "rcv", None, None),
        P("src", "rcv", None),
        P("src", "rcv", None),
        P("src", "rcv", None),
        P("rcv", None),
        P(),
    )
    return jax.shard_map(
        functools.partial(on_device, nj, ny, nz),
        mesh=mesh,
        in_specs=placed,
        out_specs=(P("src", None), P("rcv", None), P(), P("src", "rcv", None, None)),
        check_vma=False,
    )
```

```python
import functools

import jax
import jax.numpy as jnp
import ml_dtypes
import numpy as np
from jax import lax
from jax.experimental import pallas as pl
from jax.experimental.pallas import tpu as pltpu
from jax.sharding import PartitionSpec as P

NSRC = 32
NRCV = 32
NOFF = 64
ROWS = NSRC + NRCV + NOFF
MESH = pl.DeviceIdType.MESH
OVER_LANES = (((1,), (1,)), ((), ()))


def dft_tables(samples, bins, chunks):
    times = np.arange(samples, dtype=np.int64)[:, None]
    freqs = np.arange(bins, dtype=np.int64)[None, :]
    phase = (times * freqs) % samples
    angle = phase.astype(np.float32) * np.float32(2.0 * 3.141592653589793 / samples)
    cosine = np.cos(angle).astype(ml_dtypes.bfloat16)
    sine = (-np.sin(angle)).astype(ml_dtypes.bfloat16)
    width = bins // chunks
    return np.stack(
        [
            np.concatenate([t[:, c * width : (c + 1) * width] for t in (cosine, sine)], axis=1)
            for c in range(chunks)
        ]
    )


def hot_rows(src, rcv, off):
    parts = []
    for ids, count in ((src, NSRC), (rcv, NRCV), (off, NOFF)):
        rows = lax.broadcasted_iota(jnp.int32, (count, ids.shape[1]), 0)
        parts.append((rows == ids).astype(jnp.float32))
    return jnp.concatenate(parts, axis=0)


def split(values):
    high = values.astype(jnp.bfloat16)
    low = (values - high.astype(jnp.float32)).astype(jnp.bfloat16)
    return high, low


def dot(a, b):
    return jnp.dot(a, b, preferred_element_type=jnp.float32)


def tiles_of(values, count):
    return [values[:, t * ROWS : (t + 1) * ROWS] for t in range(count)]


def pick(tiles, lane):
    out = pltpu.roll(tiles[0], ROWS - 32, 1)
    out = jnp.where(lane < 32, out, tiles[1])
    out = jnp.where(lane < 64, out, pltpu.roll(tiles[2], 32, 1))
    return jnp.where(lane < 96, out, pltpu.roll(tiles[3], 64, 1))


HALVES = 2


def add(values):
    return functools.reduce(lambda a, b: a + b, values)


def sweep_kernel(
    nj, ny, nz, groups,
    traces_hbm, tables_hbm, src_hbm, rcv_hbm, off_hbm, rinit_hbm, oinit_hbm,
    spectra_hbm, terms_hbm, hot_hbm,
    traces_buf, tables_buf, ids_buf, init_buf, shift_buf, x_buf, hot_buf, sums_buf,
    gy_buf, gz_buf, gr_buf, a_buf, s_buf, flat_buf, p_buf, b1_buf, b2_buf, t_buf, c_buf, d_out,
    load_sem, table_sem, store_sem, send_sem, recv_sem,
):
    i = lax.axis_index("src")
    j = lax.axis_index("rcv")
    y = i // nz
    z = lax.rem(i, nz)
    samples = traces_buf.shape[1]
    width = x_buf.shape[2]
    per = a_buf.shape[2]
    few = per // ny
    quarter = per // 4
    tiles = nj * NRCV // ROWS
    each = nj // groups
    first = j // each

    mine = ids_buf.at[j]
    loads = [
        pltpu.make_async_copy(src_hbm, mine.at[0], load_sem.at[0]),
        pltpu.make_async_copy(rcv_hbm, mine.at[1], load_sem.at[1]),
        pltpu.make_async_copy(off_hbm, mine.at[2], load_sem.at[2]),
        pltpu.make_async_copy(traces_hbm, traces_buf, load_sem.at[3]),
        pltpu.make_async_copy(rinit_hbm, init_buf.at[pl.ds(NSRC, NRCV)], load_sem.at[4]),
        pltpu.make_async_copy(oinit_hbm, init_buf.at[pl.ds(NSRC + NRCV, NOFF)], load_sem.at[5]),
    ]
    order = [h * groups + lax.rem(first + k, groups) for h in range(HALVES) for k in range(groups)]
    tables = [
        pltpu.make_async_copy(tables_hbm.at[c], tables_buf.at[c], table_sem.at[k])
        for k, c in enumerate(order)
    ]
    for copy in loads[:4] + tables[:1] + loads[4:] + tables[1:]:
        copy.start()

    def over_j(d):
        peer = lax.rem(j + d, nj)
        return peer, (i, peer)

    def over_y(d):
        peer = lax.rem(y + d, ny)
        return peer, (peer * nz + z, j)

    def over_z(d):
        peer = lax.rem(z + d, nz)
        return peer, (y * nz + peer, j)

    def copy_to(device, source, target, phase):
        return pltpu.make_async_remote_copy(
            src_ref=source, dst_ref=target, send_sem=send_sem.at[phase],
            recv_sem=recv_sem.at[phase], device_id=device, device_id_type=MESH,
        )

    def send(n, over, me, source, buf, phase):
        for d in range(1, n):
            peer, device = over(d)
            copy_to(device, source(peer), buf.at[me], phase).start()

    def all_of(n, over, buf, phase):
        part = buf.at[pl.ds(0, n - 1)]
        return copy_to(over(1)[1], part, part, phase)

    barrier = pltpu.get_barrier_semaphore()
    for n, over in ((ny, over_y), (nj, over_j), (nz, over_z)):
        for d in range(1, n):
            pl.semaphore_signal(barrier, inc=1, device_id=over(d)[1], device_id_type=MESH)

    for copy in loads[:3]:
        copy.wait()
    hot = hot_rows(ids_buf[j, 0], ids_buf[j, 1], ids_buf[j, 2])
    hot_buf[...] = hot.T.astype(jnp.bfloat16)
    hot = hot.astype(jnp.bfloat16)
    gram = lax.dot_general(hot, hot, OVER_LANES, preferred_element_type=jnp.float32)
    gy_buf[y] = gram[NSRC : NSRC + NRCV]
    row = lax.broadcasted_iota(jnp.int32, (ROWS, ROWS), 0)
    lane = lax.broadcasted_iota(jnp.int32, (ROWS, ROWS), 1)
    from_rcv = (lane >= NSRC) & (lane < NSRC + NRCV) & (row < NSRC)
    from_off = (lane >= NSRC + NRCV) & (row < NSRC + NRCV)
    before = jnp.where(from_rcv | from_off, gram, 0.0).astype(jnp.bfloat16)
    pl.semaphore_wait(barrier, nj + ny + nz - 3)
    send(nj, over_j, j, lambda p: ids_buf.at[j], ids_buf, 0)
    stores = [pltpu.make_async_copy(hot_buf, hot_hbm, load_sem.at[0])]
    stores[0].start()

    for copy in loads[4:]:
        copy.wait()
    init_buf[:NSRC] = jnp.zeros((NSRC, init_buf.shape[1]), jnp.float32)
    shift_buf[...] = dot(
        jnp.concatenate([before, before], axis=1), jnp.concatenate(split(init_buf[...]), axis=0)
    )
    loads[3].wait()
    tables[0].wait()
    ahead = dot(traces_buf[...], tables_buf[order[0]])
    for n, c in enumerate(order):
        h, k = n // groups, n % groups
        g = c - h * groups
        both = ahead
        if n + 1 < len(order):
            tables[n + 1].wait()
            ahead = dot(traces_buf[...], tables_buf[order[n + 1]])
        real, imag = both[:, :width], both[:, width:]
        spectra = 0.5 * jnp.log((real * real + imag * imag) * (1.0 / samples) + 0.25)
        x_buf[c] = spectra
        store = pltpu.make_async_copy(x_buf.at[c], spectra_hbm.at[c], store_sem.at[n])
        store.start()
        stores.append(store)
        spec_high, spec_low = split(spectra)
        span = pl.ds(pl.multiple_of(c * width, width), width)
        sums = dot(hot, spec_high) + dot(hot, spec_low) - shift_buf[:, span]
        turned = sums.T
        for q in range(each):
            sums_buf[h, g * each + q] = turned[q * per : (q + 1) * per]
        for q in range(1 if k == 0 else 0, each):
            peer = g * each + (lax.rem(j + q, each) if k == 0 else q)
            copy_to((i, peer), sums_buf.at[h, peer], a_buf.at[h, j], 4 + 5 * h).start()
        if n == groups - 1:
            send(ny, over_y, y, lambda p: gy_buf.at[y], gy_buf, 1)
    for h in range(HALVES):
        a_buf[h, j] = sums_buf[h, j]

    all_of(nj, over_j, ids_buf, 0).wait_recv()
    by_src = []
    for q in range(nj):
        peer_hot = hot_rows(ids_buf[q, 0], ids_buf[q, 1], ids_buf[q, 2]).astype(jnp.bfloat16)
        by_src.append(
            lax.dot_general(
                peer_hot[:NSRC], peer_hot, OVER_LANES, preferred_element_type=jnp.float32
            )
        )
    src_count = add(by_src)
    n_src = jnp.sum(src_count, axis=0, keepdims=True) + 1.0
    off_high, off_low = split(src_count)
    counts = [
        pick(by_src[4 * t : 4 * t + 4], lane[:NSRC]).astype(jnp.bfloat16) for t in range(tiles)
    ]
    counts = jnp.concatenate(counts + [off_high, off_low], axis=1)
    lane = lane[:per]
    all_of(ny, over_y, gy_buf, 1).wait_recv()
    gz_buf[z] = jnp.sum(gy_buf[...], axis=0)
    send(nz, over_z, z, lambda p: gz_buf.at[z], gz_buf, 2)

    def source_step(h):
        all_of(nj, over_j, a_buf.at[h], 4 + 5 * h).wait_recv()
        parts = [a_buf[h, q] for q in range(nj)]
        total = add(parts)
        src_terms = jnp.where(lane < NSRC, total / n_src, 0.0)
        both = dot(jnp.concatenate(split(src_terms[:, :NSRC]), axis=0), counts)
        along = tiles_of(both[:per] + both[per:], tiles + 2)
        for t in range(tiles):
            left = pick(parts[4 * t : 4 * t + 4], lane) - along[t]
            flat_buf[h, :, t * ROWS : (t + 1) * ROWS] = left
        flat_buf[h, :, tiles * ROWS :] = total - along[tiles] - along[tiles + 1]
        for q in range(ny):
            p_buf[h, q] = flat_buf[h, q * few : (q + 1) * few, :]
        send(ny, over_y, y, lambda p: p_buf.at[h, p], b1_buf.at[h], 5 + 5 * h)
        b1_buf[h, y] = p_buf[h, y]
        groups_of = [src_terms[q * quarter : (q + 1) * quarter] for q in range(4)]
        s_buf[h] = add([groups_of[0]] + [pltpu.roll(groups_of[q], 32 * q, 1) for q in (1, 2, 3)])

    def reduce_step(h):
        all_of(ny, over_y, b1_buf.at[h], 5 + 5 * h).wait_recv()
        b2_buf[h, z] = add([b1_buf[h, q] for q in range(ny)])
        send(nz, over_z, z, lambda p: b2_buf.at[h, z], b2_buf.at[h], 6 + 5 * h)

    def term_step(h):
        all_of(nz, over_z, b2_buf.at[h], 6 + 5 * h).wait_recv()
        reduced = add([b2_buf[h, q] for q in range(nz)])
        rcv_terms = reduced[:, : tiles * ROWS] / n_rcv
        for k, part in enumerate(split(rcv_terms)):
            t_buf[h, k * few : (k + 1) * few, :] = part.astype(jnp.float32)
        both = dot(t_buf[h].astype(jnp.bfloat16), by_rcv)
        both = both[:few] + both[few:]
        later = reduced[:, tiles * ROWS :] - both[:, :ROWS] - both[:, ROWS:]
        c_buf[h, y] = jnp.concatenate([rcv_terms, later / n_off], axis=1)
        send(ny, over_y, y, lambda p: c_buf.at[h, y], c_buf.at[h], 7 + 5 * h)

    def source_out(h):
        send(
            nj, over_j, j, lambda p: s_buf.at[h],
            terms_hbm.at[h, :, pl.ds(3 * quarter, quarter)], 4 + 5 * HALVES + h,
        )
        own = pltpu.make_async_copy(
            s_buf.at[h], terms_hbm.at[h, j, pl.ds(3 * quarter, quarter)], load_sem.at[3 + h]
        )
        own.start()
        stores.append(own)

    def back_step(h):
        all_of(ny, over_y, c_buf.at[h], 7 + 5 * h).wait_recv()
        for q in range(ny):
            flat_buf[h, q * few : (q + 1) * few, :] = c_buf[h, q]
        off_tile = flat_buf[h, :, tiles * ROWS :]
        off_fill = [pltpu.roll(off_tile[3 * quarter :], shift, 1) for shift in (64, 32)]
        for t in range(tiles):
            tile = flat_buf[h, :, t * ROWS : (t + 1) * ROWS]
            for q in range(4):
                turned = tile if q == 1 else pltpu.roll(tile, (32 - 32 * q) % ROWS, 1)
                fill = [pltpu.roll(turned[3 * quarter :], 96, 1)] + off_fill
                whole = jnp.where(lane < NSRC + NRCV, turned, off_tile)
                for k in range(3):
                    rows = slice(k * quarter, (k + 1) * quarter)
                    d_out[h, 4 * t + q, rows, :] = jnp.where(
                        lane[:quarter] < 32, fill[k], whole[rows]
                    )
        back = terms_hbm.at[h, :, pl.ds(0, 3 * quarter)]
        send(nj, over_j, j, lambda p: d_out.at[h, p], back, 8 + 5 * h)
        own = pltpu.make_async_copy(d_out.at[h, j], back.at[j], load_sem.at[1 + h])
        own.start()
        stores.append(own)

    source_step(0)
    source_step(1)
    all_of(nz, over_z, gz_buf, 2).wait_recv()
    count = jnp.sum(gz_buf[...], axis=0)
    half = NRCV // 2
    wide = lax.broadcasted_iota(jnp.int32, (half, ROWS), 1) >= NSRC + NRCV
    gr_buf[j] = jnp.where(wide, count[:half], pltpu.roll(count[half:], ROWS // 2, 1))
    send(nj, over_j, j, lambda p: gr_buf.at[j], gr_buf, 3)
    for h in range(HALVES):
        source_out(h)
    reduce_step(0)
    reduce_step(1)

    all_of(nj, over_j, gr_buf, 3).wait_recv()
    by_rcv = []
    for q in range(nj):
        packed = gr_buf[q]
        by_rcv.append(jnp.where(wide, packed, 0.0))
        by_rcv.append(jnp.where(wide, pltpu.roll(packed, ROWS // 2, 1), 0.0))
    by_rcv = jnp.concatenate(by_rcv, axis=0)
    n_off = jnp.sum(by_rcv, axis=0, keepdims=True) + 1.0
    by_rcv = split(by_rcv)
    ones = jnp.ones((16, ROWS), jnp.bfloat16)
    n_rcv = add(
        [
            lax.dot_general(ones, part, OVER_LANES, preferred_element_type=jnp.float32)
            for part in by_rcv
        ]
    )[:1] + 1.0
    by_rcv = jnp.concatenate(by_rcv, axis=1)

    term_step(0)
    term_step(1)
    back_step(0)
    back_step(1)

    for phase, (n, over, buf) in enumerate(
        [(nj, over_j, ids_buf), (ny, over_y, gy_buf), (nz, over_z, gz_buf), (nj, over_j, gr_buf)]
    ):
        all_of(n, over, buf, phase).wait_send()
    for h in range(HALVES):
        for phase, (n, over, buf) in enumerate(
            [
                (nj, over_j, a_buf), (ny, over_y, b1_buf), (nz, over_z, b2_buf),
                (ny, over_y, c_buf), (nj, over_j, d_out),
            ]
        ):
            all_of(n, over, buf.at[h], 4 + 5 * h + phase).wait_send()
        sources = terms_hbm.at[h, :, pl.ds(3 * quarter, quarter)]
        all_of(nj, over_j, sources, 4 + 5 * HALVES + h).wait_send()
        all_of(nj, over_j, sources, 4 + 5 * HALVES + h).wait_recv()
    for store in stores:
        store.wait()
    for h in range(HALVES):
        all_of(nj, over_j, terms_hbm.at[h, :, pl.ds(0, 3 * quarter)], 8 + 5 * h).wait_recv()


def sweep(traces, src, rcv, off, receiver_init, offset_init, nj, ny, nz):
    traces_n, samples = traces.shape
    bins = receiver_init.shape[1]
    groups = max(1, bins // (256 * HALVES))
    chunks = HALVES * groups
    width = bins // chunks
    per = bins // nj // HALVES
    few = per // ny
    wide = nj * NRCV + ROWS
    f32, b16 = jnp.float32, jnp.bfloat16
    tables = jnp.asarray(dft_tables(samples, bins, chunks))
    anywhere = pl.BlockSpec(memory_space=pl.ANY)
    dma = pltpu.SemaphoreType.DMA
    phases = 4 + 6 * HALVES
    return pl.pallas_call(
        functools.partial(sweep_kernel, nj, ny, nz, groups),
        in_specs=[anywhere] * 7,
        out_specs=[anywhere] * 3,
        out_shape=[
            jax.ShapeDtypeStruct((chunks, traces_n, width), f32),
            jax.ShapeDtypeStruct((HALVES, nj, per, ROWS), f32),
            jax.ShapeDtypeStruct((traces_n, ROWS), b16),
        ],
        scratch_shapes=[
            pltpu.VMEM((traces_n, samples), b16),
            pltpu.VMEM((chunks, samples, 2 * width), b16),
            pltpu.VMEM((nj, 3, 1, traces_n), jnp.int32),
            pltpu.VMEM((ROWS, bins), f32),
            pltpu.VMEM((ROWS, bins), f32),
            pltpu.VMEM((chunks, traces_n, width), f32),
            pltpu.VMEM((traces_n, ROWS), b16),
            pltpu.VMEM((HALVES, nj, per, ROWS), f32),
            pltpu.VMEM((ny, NRCV, ROWS), f32),
            pltpu.VMEM((nz, NRCV, ROWS), f32),
            pltpu.VMEM((nj, NRCV // 2, ROWS), f32),
            pltpu.VMEM((HALVES, nj, per, ROWS), f32),
            pltpu.VMEM((HALVES, per // 4, ROWS), f32),
            pltpu.VMEM((HALVES, per, wide), f32),
            pltpu.VMEM((HALVES, ny, few, wide), f32),
            pltpu.VMEM((HALVES, ny, few, wide), f32),
            pltpu.VMEM((HALVES, nz, few, wide), f32),
            pltpu.VMEM((HALVES, 2 * few, nj * NRCV), f32),
            pltpu.VMEM((HALVES, ny, few, wide), f32),
            pltpu.VMEM((HALVES, nj, per // 4 * 3, ROWS), f32),
            dma((6,)), dma((chunks,)), dma((chunks,)), dma((phases,)), dma((phases,)),
        ],
        compiler_params=pltpu.CompilerParams(
            collective_id=0, has_side_effects=True, vmem_limit_bytes=60 * 1024 * 1024
        ),
    )(traces, tables, src, rcv, off, receiver_init, offset_init)


def unpack(packed, per):
    quarter = per // 4
    lane = lax.broadcasted_iota(jnp.int32, (quarter, ROWS), 1)
    out = []
    for start in range(0, packed.shape[0], per):
        rows = [packed[start + k * quarter : start + (k + 1) * quarter] for k in range(4)]
        sources = rows[3]
        out.append(jnp.where(lane < 32, sources, rows[0]))
        out.append(jnp.where(lane < 32, pltpu.roll(sources, 96, 1), rows[1]))
        out.append(jnp.where(lane < 32, pltpu.roll(sources, 64, 1), rows[2]))
        last = jnp.where(lane < 96, pltpu.roll(rows[1], 64, 1), pltpu.roll(rows[2], 96, 1))
        last = jnp.where(lane < 64, pltpu.roll(rows[0], 32, 1), last)
        out.append(jnp.where(lane < 32, pltpu.roll(sources, 32, 1), last))
    return jnp.concatenate(out, axis=0)


def finish_kernel(
    per, hot_hbm, spectra_hbm, turned_hbm, src_out, rcv_out, off_out, residual_out,
    hot_buf, x_buf, turned_buf, terms_buf, load_sem, x_sem, turned_sem, store_sem, out_sem,
):
    chunks, _, width = x_buf.shape
    load = pltpu.make_async_copy(hot_hbm, hot_buf, load_sem.at[0])
    load.start()
    parts = []
    for c in range(chunks):
        rows = pl.ds(c * width, width)
        parts.append((
            pltpu.make_async_copy(turned_hbm.at[rows], turned_buf.at[rows], turned_sem.at[c]),
            pltpu.make_async_copy(spectra_hbm.at[c], x_buf.at[c], x_sem.at[c]),
        ))
        for copy in parts[c]:
            copy.start()
    load.wait()
    hot = jnp.concatenate([hot_buf[...]] * 2, axis=1)
    stores = []
    for c in range(chunks):
        for copy in parts[c]:
            copy.wait()
        span = slice(c * width, (c + 1) * width)
        turned = unpack(turned_buf[span], per)
        both = jnp.concatenate(split(turned), axis=1)
        spread = lax.dot_general(hot, both, OVER_LANES, preferred_element_type=jnp.float32)
        x_buf[c] = x_buf[c] - spread
        store = pltpu.make_async_copy(
            x_buf.at[c], residual_out.at[0, 0, :, pl.ds(c * width, width)], store_sem.at[c]
        )
        store.start()
        stores.append(store)
        terms_buf[:, span] = turned.T
    start = 0
    for k, (out, count) in enumerate(((src_out, NSRC), (rcv_out, NRCV), (off_out, NOFF))):
        store = pltpu.make_async_copy(terms_buf.at[pl.ds(start, count)], out, out_sem.at[k])
        store.start()
        stores.append(store)
        start += count
    for store in stores:
        store.wait()


def finish(hot, spectra, turned, per):
    chunks, traces_n, width = spectra.shape
    bins = chunks * width
    f32 = jnp.float32
    anywhere = pl.BlockSpec(memory_space=pl.ANY)
    dma = pltpu.SemaphoreType.DMA
    return pl.pallas_call(
        functools.partial(finish_kernel, per),
        in_specs=[anywhere] * 3,
        out_specs=[anywhere] * 4,
        out_shape=[
            jax.ShapeDtypeStruct((NSRC, bins), f32),
            jax.ShapeDtypeStruct((NRCV, bins), f32),
            jax.ShapeDtypeStruct((NOFF, bins), f32),
            jax.ShapeDtypeStruct((1, 1, traces_n, bins), f32),
        ],
        scratch_shapes=[
            pltpu.VMEM(hot.shape, hot.dtype),
            pltpu.VMEM(spectra.shape, f32),
            pltpu.VMEM(turned.shape, f32),
            pltpu.VMEM((ROWS, bins), f32),
            dma((1,)), dma((chunks,)), dma((chunks,)), dma((chunks,)), dma((3,)),
        ],
        compiler_params=pltpu.CompilerParams(vmem_limit_bytes=60 * 1024 * 1024),
    )(hot, spectra, turned)


def on_device(
    nj, ny, nz, traces, source_ids, receiver_ids, offset_ids, receiver_init, offset_init
):
    src, rcv, off = source_ids[0], receiver_ids[0], offset_ids[0]
    spectra, turned, hot = sweep(
        traces[0, 0], src, rcv, off, receiver_init, offset_init, nj, ny, nz
    )
    return finish(hot, spectra, turned.reshape(-1, ROWS), turned.shape[2])


def solution(mesh):
    nsrc, nj = mesh.shape["src"], mesh.shape["rcv"]
    nz = 4 if nsrc >= 32 else 2
    ny = nsrc // nz
    placed = (
        P("src", "rcv", None, None),
        P("src", "rcv", None),
        P("src", "rcv", None),
        P("src", "rcv", None),
        P("rcv", None),
        P(),
    )
    return jax.shard_map(
        functools.partial(on_device, nj, ny, nz),
        mesh=mesh,
        in_specs=placed,
        out_specs=(P("src", None), P("rcv", None), P(), P("src", "rcv", None, None)),
        check_vma=False,
    )
```

```python
import functools

import jax
import jax.numpy as jnp
import ml_dtypes
import numpy as np
from jax import lax
from jax.experimental import pallas as pl
from jax.experimental.pallas import tpu as pltpu
from jax.sharding import PartitionSpec as P

NSRC = 32
NRCV = 32
NOFF = 64
ROWS = NSRC + NRCV + NOFF
MESH = pl.DeviceIdType.MESH
OVER_LANES = (((1,), (1,)), ((), ()))


def dft_tables(samples, bins, chunks):
    times = np.arange(samples, dtype=np.int64)[:, None]
    freqs = np.arange(bins, dtype=np.int64)[None, :]
    phase = (times * freqs) % samples
    angle = phase.astype(np.float32) * np.float32(2.0 * 3.141592653589793 / samples)
    cosine = np.cos(angle).astype(ml_dtypes.bfloat16)
    sine = (-np.sin(angle)).astype(ml_dtypes.bfloat16)
    width = bins // chunks
    return np.stack(
        [
            np.concatenate([t[:, c * width : (c + 1) * width] for t in (cosine, sine)], axis=1)
            for c in range(chunks)
        ]
    )


def hot_rows(src, rcv, off):
    parts = []
    for ids, count in ((src, NSRC), (rcv, NRCV), (off, NOFF)):
        rows = lax.broadcasted_iota(jnp.int32, (count, ids.shape[1]), 0)
        parts.append((rows == ids).astype(jnp.float32))
    return jnp.concatenate(parts, axis=0)


def split(values):
    high = values.astype(jnp.bfloat16)
    low = (values - high.astype(jnp.float32)).astype(jnp.bfloat16)
    return high, low


def dot(a, b):
    return jnp.dot(a, b, preferred_element_type=jnp.float32)


def tiles_of(values, count):
    return [values[:, t * ROWS : (t + 1) * ROWS] for t in range(count)]


def pick(tiles, lane):
    out = pltpu.roll(tiles[0], ROWS - 32, 1)
    out = jnp.where(lane < 32, out, tiles[1])
    out = jnp.where(lane < 64, out, pltpu.roll(tiles[2], 32, 1))
    return jnp.where(lane < 96, out, pltpu.roll(tiles[3], 64, 1))


HALVES = 2


def add(values):
    return functools.reduce(lambda a, b: a + b, values)


def sweep_kernel(
    nj, ny, nz, groups,
    traces_hbm, tables_hbm, src_hbm, rcv_hbm, off_hbm, rinit_hbm, oinit_hbm,
    spectra_hbm, terms_hbm, hot_hbm,
    traces_buf, tables_buf, ids_buf, init_buf, shift_buf, x_buf, hot_buf, sums_buf,
    gy_buf, gz_buf, gr_buf, a_buf, s_buf, flat_buf, p_buf, b1_buf, b2_buf, t_buf, c_buf, d_out,
    load_sem, table_sem, store_sem, send_sem, recv_sem,
):
    i = lax.axis_index("src")
    j = lax.axis_index("rcv")
    y = i // nz
    z = lax.rem(i, nz)
    samples = traces_buf.shape[1]
    width = x_buf.shape[2]
    per = a_buf.shape[2]
    few = per // ny
    quarter = per // 4
    tiles = nj * NRCV // ROWS
    each = nj // groups
    first = j // each

    mine = ids_buf.at[j]
    loads = [
        pltpu.make_async_copy(src_hbm, mine.at[0], load_sem.at[0]),
        pltpu.make_async_copy(rcv_hbm, mine.at[1], load_sem.at[1]),
        pltpu.make_async_copy(off_hbm, mine.at[2], load_sem.at[2]),
        pltpu.make_async_copy(traces_hbm, traces_buf, load_sem.at[3]),
        pltpu.make_async_copy(rinit_hbm, init_buf.at[pl.ds(NSRC, NRCV)], load_sem.at[4]),
        pltpu.make_async_copy(oinit_hbm, init_buf.at[pl.ds(NSRC + NRCV, NOFF)], load_sem.at[5]),
    ]
    order = [h * groups + lax.rem(first + k, groups) for h in range(HALVES) for k in range(groups)]
    tables = [
        pltpu.make_async_copy(tables_hbm.at[c], tables_buf.at[c], table_sem.at[k])
        for k, c in enumerate(order)
    ]
    for copy in loads[:4] + tables[:1] + loads[4:] + tables[1:]:
        copy.start()

    def over_j(d):
        peer = lax.rem(j + d, nj)
        return peer, (i, peer)

    def over_y(d):
        peer = lax.rem(y + d, ny)
        return peer, (peer * nz + z, j)

    def over_z(d):
        peer = lax.rem(z + d, nz)
        return peer, (y * nz + peer, j)

    def copy_to(device, source, target, phase):
        return pltpu.make_async_remote_copy(
            src_ref=source, dst_ref=target, send_sem=send_sem.at[phase],
            recv_sem=recv_sem.at[phase], device_id=device, device_id_type=MESH,
        )

    def send(n, over, me, source, buf, phase):
        for d in range(1, n):
            peer, device = over(d)
            copy_to(device, source(peer), buf.at[me], phase).start()

    def all_of(n, over, buf, phase):
        part = buf.at[pl.ds(0, n - 1)]
        return copy_to(over(1)[1], part, part, phase)

    barrier = pltpu.get_barrier_semaphore()
    for n, over in ((ny, over_y), (nj, over_j), (nz, over_z)):
        for d in range(1, n):
            pl.semaphore_signal(barrier, inc=1, device_id=over(d)[1], device_id_type=MESH)

    for copy in loads[:3]:
        copy.wait()
    hot = hot_rows(ids_buf[j, 0], ids_buf[j, 1], ids_buf[j, 2])
    hot_buf[...] = hot.T.astype(jnp.bfloat16)
    hot = hot.astype(jnp.bfloat16)
    gram = lax.dot_general(hot, hot, OVER_LANES, preferred_element_type=jnp.float32)
    gy_buf[y] = gram[NSRC : NSRC + NRCV]
    row = lax.broadcasted_iota(jnp.int32, (ROWS, ROWS), 0)
    lane = lax.broadcasted_iota(jnp.int32, (ROWS, ROWS), 1)
    from_rcv = (lane >= NSRC) & (lane < NSRC + NRCV) & (row < NSRC)
    from_off = (lane >= NSRC + NRCV) & (row < NSRC + NRCV)
    before = jnp.where(from_rcv | from_off, gram, 0.0).astype(jnp.bfloat16)
    pl.semaphore_wait(barrier, nj + ny + nz - 3)
    send(nj, over_j, j, lambda p: ids_buf.at[j], ids_buf, 0)
    stores = [pltpu.make_async_copy(hot_buf, hot_hbm, load_sem.at[0])]
    stores[0].start()

    for copy in loads[4:]:
        copy.wait()
    init_buf[:NSRC] = jnp.zeros((NSRC, init_buf.shape[1]), jnp.float32)
    shift_buf[...] = dot(
        jnp.concatenate([before, before], axis=1), jnp.concatenate(split(init_buf[...]), axis=0)
    )
    loads[3].wait()
    tables[0].wait()
    ahead = dot(traces_buf[...], tables_buf[order[0]])
    for n, c in enumerate(order):
        h, k = n // groups, n % groups
        g = c - h * groups
        both = ahead
        if n + 1 < len(order):
            tables[n + 1].wait()
            ahead = dot(traces_buf[...], tables_buf[order[n + 1]])
        real, imag = both[:, :width], both[:, width:]
        spectra = 0.5 * jnp.log((real * real + imag * imag) * (1.0 / samples) + 0.25)
        x_buf[c] = spectra
        store = pltpu.make_async_copy(x_buf.at[c], spectra_hbm.at[c], store_sem.at[n])
        store.start()
        stores.append(store)
        spec_high, spec_low = split(spectra)
        span = pl.ds(pl.multiple_of(c * width, width), width)
        sums = dot(hot, spec_high) + dot(hot, spec_low) - shift_buf[:, span]
        turned = sums.T
        for q in range(each):
            sums_buf[h, g * each + q] = turned[q * per : (q + 1) * per]
        for q in range(1 if k == 0 else 0, each):
            peer = g * each + (lax.rem(j + q, each) if k == 0 else q)
            copy_to((i, peer), sums_buf.at[h, peer], a_buf.at[h, j], 4 + 5 * h).start()
        if n == groups - 1:
            send(ny, over_y, y, lambda p: gy_buf.at[y], gy_buf, 1)
    for h in range(HALVES):
        a_buf[h, j] = sums_buf[h, j]

    all_of(nj, over_j, ids_buf, 0).wait_recv()
    by_src = []
    for q in range(nj):
        peer_hot = hot_rows(ids_buf[q, 0], ids_buf[q, 1], ids_buf[q, 2]).astype(jnp.bfloat16)
        by_src.append(
            lax.dot_general(
                peer_hot[:NSRC], peer_hot, OVER_LANES, preferred_element_type=jnp.float32
            )
        )
    src_count = add(by_src)
    n_src = jnp.sum(src_count, axis=0, keepdims=True) + 1.0
    off_high, off_low = split(src_count)
    counts = [
        pick(by_src[4 * t : 4 * t + 4], lane[:NSRC]).astype(jnp.bfloat16) for t in range(tiles)
    ]
    counts = jnp.concatenate(counts + [off_high, off_low], axis=1)
    lane = lane[:per]
    all_of(ny, over_y, gy_buf, 1).wait_recv()
    gz_buf[z] = jnp.sum(gy_buf[...], axis=0)
    send(nz, over_z, z, lambda p: gz_buf.at[z], gz_buf, 2)

    def source_step(h):
        all_of(nj, over_j, a_buf.at[h], 4 + 5 * h).wait_recv()
        parts = [a_buf[h, q] for q in range(nj)]
        total = add(parts)
        src_terms = jnp.where(lane < NSRC, total / n_src, 0.0)
        both = dot(jnp.concatenate(split(src_terms[:, :NSRC]), axis=0), counts)
        along = tiles_of(both[:per] + both[per:], tiles + 2)
        for t in range(tiles):
            left = pick(parts[4 * t : 4 * t + 4], lane) - along[t]
            flat_buf[h, :, t * ROWS : (t + 1) * ROWS] = left
        flat_buf[h, :, tiles * ROWS :] = total - along[tiles] - along[tiles + 1]
        for q in range(ny):
            p_buf[h, q] = flat_buf[h, q * few : (q + 1) * few, :]
        send(ny, over_y, y, lambda p: p_buf.at[h, p], b1_buf.at[h], 5 + 5 * h)
        b1_buf[h, y] = p_buf[h, y]
        groups_of = [src_terms[q * quarter : (q + 1) * quarter] for q in range(4)]
        s_buf[h] = add([groups_of[0]] + [pltpu.roll(groups_of[q], 32 * q, 1) for q in (1, 2, 3)])

    def reduce_step(h):
        all_of(ny, over_y, b1_buf.at[h], 5 + 5 * h).wait_recv()
        b2_buf[h, z] = add([b1_buf[h, q] for q in range(ny)])
        send(nz, over_z, z, lambda p: b2_buf.at[h, z], b2_buf.at[h], 6 + 5 * h)

    def term_step(h):
        all_of(nz, over_z, b2_buf.at[h], 6 + 5 * h).wait_recv()
        reduced = add([b2_buf[h, q] for q in range(nz)])
        rcv_terms = reduced[:, : tiles * ROWS] / n_rcv
        for k, part in enumerate(split(rcv_terms)):
            t_buf[h, k * few : (k + 1) * few, :] = part.astype(jnp.float32)
        both = dot(t_buf[h].astype(jnp.bfloat16), by_rcv)
        both = both[:few] + both[few:]
        later = reduced[:, tiles * ROWS :] - both[:, :ROWS] - both[:, ROWS:]
        c_buf[h, y] = jnp.concatenate([rcv_terms, later / n_off], axis=1)
        send(ny, over_y, y, lambda p: c_buf.at[h, y], c_buf.at[h], 7 + 5 * h)

    def source_part(place):
        return terms_hbm.at[:, place, pl.ds(3 * quarter, quarter)]

    def sources_sent():
        part = source_part(pl.ds(0, nj - 1))
        return copy_to(over_j(1)[1], part, part, 4 + 5 * HALVES)

    def source_out():
        for d in range(1, nj):
            copy_to(over_j(d)[1], s_buf, source_part(j), 4 + 5 * HALVES).start()
        own = pltpu.make_async_copy(s_buf, source_part(j), load_sem.at[3])
        own.start()
        stores.append(own)

    def back_step(h):
        all_of(ny, over_y, c_buf.at[h], 7 + 5 * h).wait_recv()
        for q in range(ny):
            flat_buf[h, q * few : (q + 1) * few, :] = c_buf[h, q]
        off_tile = flat_buf[h, :, tiles * ROWS :]
        off_fill = [pltpu.roll(off_tile[3 * quarter :], shift, 1) for shift in (64, 32)]
        for t in range(tiles):
            tile = flat_buf[h, :, t * ROWS : (t + 1) * ROWS]
            for q in range(4):
                turned = tile if q == 1 else pltpu.roll(tile, (32 - 32 * q) % ROWS, 1)
                fill = [pltpu.roll(turned[3 * quarter :], 96, 1)] + off_fill
                whole = jnp.where(lane < NSRC + NRCV, turned, off_tile)
                for k in range(3):
                    rows = slice(k * quarter, (k + 1) * quarter)
                    d_out[h, 4 * t + q, rows, :] = jnp.where(
                        lane[:quarter] < 32, fill[k], whole[rows]
                    )
        back = terms_hbm.at[h, :, pl.ds(0, 3 * quarter)]
        send(nj, over_j, j, lambda p: d_out.at[h, p], back, 8 + 5 * h)
        own = pltpu.make_async_copy(d_out.at[h, j], back.at[j], load_sem.at[1 + h])
        own.start()
        stores.append(own)

    source_step(0)
    source_step(1)
    all_of(nz, over_z, gz_buf, 2).wait_recv()
    count = jnp.sum(gz_buf[...], axis=0)
    half = NRCV // 2
    wide = lax.broadcasted_iota(jnp.int32, (half, ROWS), 1) >= NSRC + NRCV
    gr_buf[j] = jnp.where(wide, count[:half], pltpu.roll(count[half:], ROWS // 2, 1))
    send(nj, over_j, j, lambda p: gr_buf.at[j], gr_buf, 3)
    reduce_step(0)
    reduce_step(1)

    all_of(nj, over_j, gr_buf, 3).wait_recv()
    by_rcv = []
    for q in range(nj):
        packed = gr_buf[q]
        by_rcv.append(jnp.where(wide, packed, 0.0))
        by_rcv.append(jnp.where(wide, pltpu.roll(packed, ROWS // 2, 1), 0.0))
    by_rcv = jnp.concatenate(by_rcv, axis=0)
    n_off = jnp.sum(by_rcv, axis=0, keepdims=True) + 1.0
    by_rcv = split(by_rcv)
    ones = jnp.ones((16, ROWS), jnp.bfloat16)
    n_rcv = add(
        [
            lax.dot_general(ones, part, OVER_LANES, preferred_element_type=jnp.float32)
            for part in by_rcv
        ]
    )[:1] + 1.0
    by_rcv = jnp.concatenate(by_rcv, axis=1)

    term_step(0)
    term_step(1)
    source_out()
    back_step(0)
    back_step(1)

    for phase, (n, over, buf) in enumerate(
        [(nj, over_j, ids_buf), (ny, over_y, gy_buf), (nz, over_z, gz_buf), (nj, over_j, gr_buf)]
    ):
        all_of(n, over, buf, phase).wait_send()
    for h in range(HALVES):
        for phase, (n, over, buf) in enumerate(
            [
                (nj, over_j, a_buf), (ny, over_y, b1_buf), (nz, over_z, b2_buf),
                (ny, over_y, c_buf), (nj, over_j, d_out),
            ]
        ):
            all_of(n, over, buf.at[h], 4 + 5 * h + phase).wait_send()
    sources_sent().wait_send()
    sources_sent().wait_recv()
    for store in stores:
        store.wait()
    for h in range(HALVES):
        all_of(nj, over_j, terms_hbm.at[h, :, pl.ds(0, 3 * quarter)], 8 + 5 * h).wait_recv()


def sweep(traces, src, rcv, off, receiver_init, offset_init, nj, ny, nz):
    traces_n, samples = traces.shape
    bins = receiver_init.shape[1]
    groups = max(1, bins // (256 * HALVES))
    chunks = HALVES * groups
    width = bins // chunks
    per = bins // nj // HALVES
    few = per // ny
    wide = nj * NRCV + ROWS
    f32, b16 = jnp.float32, jnp.bfloat16
    tables = jnp.asarray(dft_tables(samples, bins, chunks))
    anywhere = pl.BlockSpec(memory_space=pl.ANY)
    dma = pltpu.SemaphoreType.DMA
    phases = 5 + 5 * HALVES
    return pl.pallas_call(
        functools.partial(sweep_kernel, nj, ny, nz, groups),
        in_specs=[anywhere] * 7,
        out_specs=[anywhere] * 3,
        out_shape=[
            jax.ShapeDtypeStruct((chunks, traces_n, width), f32),
            jax.ShapeDtypeStruct((HALVES, nj, per, ROWS), f32),
            jax.ShapeDtypeStruct((traces_n, ROWS), b16),
        ],
        scratch_shapes=[
            pltpu.VMEM((traces_n, samples), b16),
            pltpu.VMEM((chunks, samples, 2 * width), b16),
            pltpu.VMEM((nj, 3, 1, traces_n), jnp.int32),
            pltpu.VMEM((ROWS, bins), f32),
            pltpu.VMEM((ROWS, bins), f32),
            pltpu.VMEM((chunks, traces_n, width), f32),
            pltpu.VMEM((traces_n, ROWS), b16),
            pltpu.VMEM((HALVES, nj, per, ROWS), f32),
            pltpu.VMEM((ny, NRCV, ROWS), f32),
            pltpu.VMEM((nz, NRCV, ROWS), f32),
            pltpu.VMEM((nj, NRCV // 2, ROWS), f32),
            pltpu.VMEM((HALVES, nj, per, ROWS), f32),
            pltpu.VMEM((HALVES, per // 4, ROWS), f32),
            pltpu.VMEM((HALVES, per, wide), f32),
            pltpu.VMEM((HALVES, ny, few, wide), f32),
            pltpu.VMEM((HALVES, ny, few, wide), f32),
            pltpu.VMEM((HALVES, nz, few, wide), f32),
            pltpu.VMEM((HALVES, 2 * few, nj * NRCV), f32),
            pltpu.VMEM((HALVES, ny, few, wide), f32),
            pltpu.VMEM((HALVES, nj, per // 4 * 3, ROWS), f32),
            dma((6,)), dma((chunks,)), dma((chunks,)), dma((phases,)), dma((phases,)),
        ],
        compiler_params=pltpu.CompilerParams(
            collective_id=0, has_side_effects=True, vmem_limit_bytes=60 * 1024 * 1024
        ),
    )(traces, tables, src, rcv, off, receiver_init, offset_init)


def unpack(packed, per):
    quarter = per // 4
    lane = lax.broadcasted_iota(jnp.int32, (quarter, ROWS), 1)
    out = []
    for start in range(0, packed.shape[0], per):
        rows = [packed[start + k * quarter : start + (k + 1) * quarter] for k in range(4)]
        sources = rows[3]
        out.append(jnp.where(lane < 32, sources, rows[0]))
        out.append(jnp.where(lane < 32, pltpu.roll(sources, 96, 1), rows[1]))
        out.append(jnp.where(lane < 32, pltpu.roll(sources, 64, 1), rows[2]))
        last = jnp.where(lane < 96, pltpu.roll(rows[1], 64, 1), pltpu.roll(rows[2], 96, 1))
        last = jnp.where(lane < 64, pltpu.roll(rows[0], 32, 1), last)
        out.append(jnp.where(lane < 32, pltpu.roll(sources, 32, 1), last))
    return jnp.concatenate(out, axis=0)


def finish_kernel(
    per, hot_hbm, spectra_hbm, turned_hbm, src_out, rcv_out, off_out, residual_out,
    hot_buf, x_buf, turned_buf, terms_buf, load_sem, x_sem, turned_sem, store_sem, out_sem,
):
    chunks, _, width = x_buf.shape
    load = pltpu.make_async_copy(hot_hbm, hot_buf, load_sem.at[0])
    load.start()
    parts = []
    for c in range(chunks):
        rows = pl.ds(c * width, width)
        parts.append((
            pltpu.make_async_copy(turned_hbm.at[rows], turned_buf.at[rows], turned_sem.at[c]),
            pltpu.make_async_copy(spectra_hbm.at[c], x_buf.at[c], x_sem.at[c]),
        ))
        for copy in parts[c]:
            copy.start()
    load.wait()
    hot = jnp.concatenate([hot_buf[...]] * 2, axis=1)
    stores = []
    for c in range(chunks):
        for copy in parts[c]:
            copy.wait()
        span = slice(c * width, (c + 1) * width)
        turned = unpack(turned_buf[span], per)
        both = jnp.concatenate(split(turned), axis=1)
        spread = lax.dot_general(hot, both, OVER_LANES, preferred_element_type=jnp.float32)
        x_buf[c] = x_buf[c] - spread
        store = pltpu.make_async_copy(
            x_buf.at[c], residual_out.at[0, 0, :, pl.ds(c * width, width)], store_sem.at[c]
        )
        store.start()
        stores.append(store)
        terms_buf[:, span] = turned.T
    start = 0
    for k, (out, count) in enumerate(((src_out, NSRC), (rcv_out, NRCV), (off_out, NOFF))):
        store = pltpu.make_async_copy(terms_buf.at[pl.ds(start, count)], out, out_sem.at[k])
        store.start()
        stores.append(store)
        start += count
    for store in stores:
        store.wait()


def finish(hot, spectra, turned, per):
    chunks, traces_n, width = spectra.shape
    bins = chunks * width
    f32 = jnp.float32
    anywhere = pl.BlockSpec(memory_space=pl.ANY)
    dma = pltpu.SemaphoreType.DMA
    return pl.pallas_call(
        functools.partial(finish_kernel, per),
        in_specs=[anywhere] * 3,
        out_specs=[anywhere] * 4,
        out_shape=[
            jax.ShapeDtypeStruct((NSRC, bins), f32),
            jax.ShapeDtypeStruct((NRCV, bins), f32),
            jax.ShapeDtypeStruct((NOFF, bins), f32),
            jax.ShapeDtypeStruct((1, 1, traces_n, bins), f32),
        ],
        scratch_shapes=[
            pltpu.VMEM(hot.shape, hot.dtype),
            pltpu.VMEM(spectra.shape, f32),
            pltpu.VMEM(turned.shape, f32),
            pltpu.VMEM((ROWS, bins), f32),
            dma((1,)), dma((chunks,)), dma((chunks,)), dma((chunks,)), dma((3,)),
        ],
        compiler_params=pltpu.CompilerParams(vmem_limit_bytes=60 * 1024 * 1024),
    )(hot, spectra, turned)


def on_device(
    nj, ny, nz, traces, source_ids, receiver_ids, offset_ids, receiver_init, offset_init
):
    src, rcv, off = source_ids[0], receiver_ids[0], offset_ids[0]
    spectra, turned, hot = sweep(
        traces[0, 0], src, rcv, off, receiver_init, offset_init, nj, ny, nz
    )
    return finish(hot, spectra, turned.reshape(-1, ROWS), turned.shape[2])


def solution(mesh):
    nsrc, nj = mesh.shape["src"], mesh.shape["rcv"]
    nz = 4 if nsrc >= 32 else 2
    ny = nsrc // nz
    placed = (
        P("src", "rcv", None, None),
        P("src", "rcv", None),
        P("src", "rcv", None),
        P("src", "rcv", None),
        P("rcv", None),
        P(),
    )
    return jax.shard_map(
        functools.partial(on_device, nj, ny, nz),
        mesh=mesh,
        in_specs=placed,
        out_specs=(P("src", None), P("rcv", None), P(), P("src", "rcv", None, None)),
        check_vma=False,
    )
```
